32 devices in a mesh: groups: 2 (over x), row: 16 (over z, y, core).
Axes of the slice: x: 2, y: 2, z: 4, core: 2. Of those that a mesh axis runs over, the one named last changes fastest.
Arguments:
- coupling: float32 [64, 3, 576, 576], P(('groups', 'row')), parts along dimension 0, may hold values from -0.0625 to 0.0625
- columns: int32 [64, 3], P(('groups', 'row')), parts along dimension 0, may hold values from 0 to 31, as said below
- stiff_diag: float32 [3, 12288], P(None, ('groups', 'row')), parts along dimension 1, may hold values from 0.5 to 2
- interior: int32 [12288], P(('groups', 'row')), parts along dimension 0, may hold values 0 or 1
- loads: float32 [8, 3, 12288], P(None, None, ('groups', 'row')), parts along dimension 2, may hold values from -12 to 12
Outputs:
- displacement: float32 [8, 3, 12288], P(None, None, ('groups', 'row')), parts along dimension 2
- residual: float32 [8, 3, 12288], P(None, None, ('groups', 'row')), parts along dimension 2
The draws below stay inside these ranges and needn't reach their ends.
There are 2 independent parts, one for each index of `groups`. The reference program is written for one: setup_inputs(seed, part) draws one part's arguments, and reference() takes and returns one part's arrays. A program takes and returns all parts, laid end to end along the dimension named above; each array names one. Nothing has to cross between parts.
Inputs may be any that keep to these rules, and one draw needn't show every extreme that they name: Each column of columns is a permutation of the 32 blocks, and columns[b,k] lies on the device that holds block b or on one beside it: |columns[b,k] // 2 - b // 2| <= 1.
All inputs are finite; a program needn't handle non-finite values. No bound on the sum of `interior` on one device may be relied on, other than what follows from the above.
Results may differ from the reference program's by a relative error of at most 0.0004.
Values sent between devices are 32-bit elements; how exact they have to be, the bound alone decides.
No kernel may reach another device: no remote copies, remote signals or barrier semaphores. Data moves between devices by JAX's collectives and lax.ppermute only.
A program may use at most 64 MiB of HBM per device.

```python
import math
import jax
import jax.numpy as jnp
from jax import lax

BS = 192
FIELDS = 8
KOFF = 3
ITERS = 2
BLK_DEV = 2
NBLK = 32
NODES = 6144


def draw_columns(key, part):
    block_index = jnp.arange(NBLK, dtype=jnp.int32)
    group_sizes = (2 * BLK_DEV, BLK_DEV, 2 * BLK_DEV)
    offsets = (0, BLK_DEV // 2, BLK_DEV)
    result = []
    for slot_index in range(KOFF):
        size_now = group_sizes[slot_index % 3]
        offset_now = offsets[slot_index % 3]
        group_id = (block_index + 2 * size_now - offset_now) // size_now
        jitter = jax.random.randint(jax.random.fold_in(key, slot_index), (NBLK,), 0, 1024)
        ranking = group_id * (1024 * NBLK) + jitter * NBLK + block_index
        ordered = jnp.argsort(ranking)
        result.append(ordered.astype(jnp.int32))
    return jnp.stack(result, axis=1)


def draw_loads(key, part):
    first_key = jax.random.fold_in(key, 11)
    position = jnp.arange(NODES, dtype=jnp.float32) / NODES
    values = jnp.clip(jax.random.normal(first_key, (FIELDS, 3, NODES), jnp.float32), -4.0, 4.0)
    growth = 1.0 + 2.0 * position
    return values * growth


def set_ends(values, own_key, least, top_value):
    shape = values.shape
    spot = [jax.random.randint(jax.random.fold_in(own_key, axis), (), 0, shape[axis]) for axis in range(len(shape))]
    values = values.at[tuple(spot)].set(least)
    longest = shape.index(max(shape))
    spot[longest] = (spot[longest] + 1) % shape[longest]
    return values.at[tuple(spot)].set(top_value)


def block_scale(stream_key, dims, shards, least, largest):
    def one(dim, parts):
        draws = jax.random.uniform(jax.random.fold_in(jax.random.fold_in(stream_key, 6), dim), (parts,), jnp.float32, least / len(shards), largest / len(shards))
        return jnp.repeat(jnp.exp(draws), dims[dim] // parts).reshape((-1,) + (1,) * (len(dims) - dim - 1))

    factor_of = one(*shards[0])
    for cut in shards[1:]:
        factor_of = factor_of * one(*cut)
    return factor_of


def scatter_about(stream_key, extent, scale, reach, pieces=(), kind=jnp.bfloat16):
    values = jax.random.normal(stream_key, extent, jnp.float32) * scale
    if len(pieces) > 0:
        values = block_scale(stream_key, extent, pieces, -0.22, 0.18) * values
    return jnp.clip(values, min=-reach, max=reach).astype(kind)


def setup_inputs(seed: int = 0, part: int = 0) -> dict:
    key_list = jax.random.split(jax.random.key(seed), 6)
    own_keys = jax.random.split(jax.random.fold_in(key_list[5], part), 6)
    return {
        "coupling": scatter_about(own_keys[0], (NBLK, KOFF, 3 * BS, 3 * BS), (16 * 3 * BS) ** -0.5, 0.0625, ((0, 16),), jnp.float32),
        "columns": draw_columns(jax.random.fold_in(jax.random.fold_in(key_list[5], part), 71), part),
        "stiff_diag": jnp.clip(jnp.exp(math.log(2.0) - 1.3862944 * jax.random.uniform(own_keys[2], (3, NODES), jnp.float32) ** block_scale(own_keys[2], (3, NODES), ((1, 16),), -0.2, 0.2)), 0.5, 2.0),
        "interior": set_ends((jax.random.randint(own_keys[3], (NODES,), 0, 4) < 3).astype(jnp.int32), jax.random.fold_in(own_keys[3], 1), 0, 1),
        "loads": draw_loads(jax.random.fold_in(jax.random.fold_in(key_list[5], part), 71), part),
    }


precise = lax.Precision.HIGHEST
slot_shift = 1.2

def solve_small(matrix, rhs_matrix):
    lower = jnp.linalg.cholesky(matrix)
    middle = lax.linalg.triangular_solve(lower, rhs_matrix, left_side=True, lower=True)
    return lax.linalg.triangular_solve(lower, middle, left_side=True, lower=True, transpose_a=True)

def inner_gram(left, right):
    return jnp.einsum('fcn,gcn->fg', left, right, precision=precise)

def combine(vectors, mixing):
    return jnp.einsum('gcn,gf->fcn', vectors, mixing, precision=precise)

def operate(field, coupling, columns, stiff_diag, inside):
    masked = field * inside
    blocks = masked.reshape(FIELDS, 3, NBLK, BS).transpose(2, 0, 1, 3).reshape(NBLK, FIELDS, 3 * BS)
    summed = jnp.zeros_like(blocks)
    for slot_index in range(KOFF):
        matrix = coupling[:, slot_index]
        targets = columns[:, slot_index].astype(jnp.int32)
        forward = jnp.einsum('rfj,rij->rfi', blocks[targets], matrix, precision=precise)
        reverse = jnp.einsum('rfi,rij->rfj', blocks, matrix, precision=precise)
        summed = summed + forward
        summed = summed.at[targets].add(reverse)
    spread = summed.reshape(NBLK, FIELDS, 3, BS).transpose(1, 2, 0, 3).reshape(FIELDS, 3, NODES)
    return (slot_shift * KOFF + stiff_diag) * field + inside * spread

def reference(coupling, columns, stiff_diag, interior, loads):
    inside = interior.astype(jnp.float32)
    displacement = jnp.zeros_like(loads)
    residual = loads
    direction = loads
    res_gram = inner_gram(residual, residual)
    for iteration in range(ITERS):
        image = operate(direction, coupling, columns, stiff_diag, inside)
        curvature = inner_gram(direction, image)
        step_size = solve_small(curvature, res_gram)
        displacement = displacement + combine(direction, step_size)
        residual = residual - combine(image, step_size)
        res_next = inner_gram(residual, residual)
        mixing = solve_small(res_gram, res_next)
        direction = residual + combine(direction, mixing)
        res_gram = res_next
    return (displacement, residual)
```

```python
import jax
import jax.numpy as jnp
from jax import lax
from jax.experimental import pallas as pl
from jax.experimental.pallas import tpu as pltpu
from jax.sharding import PartitionSpec as P

f32 = jnp.float32
bf16 = jnp.bfloat16
precise = lax.Precision.HIGHEST
slot_shift = 1.2
diag_middle = 1.25


def call(body, out_shape, in_specs, scratch=(), flops=0, name=None):
    return pl.pallas_call(
        body,
        out_shape=out_shape,
        in_specs=in_specs,
        out_specs=jax.tree.map(lambda _: pl.BlockSpec(memory_space=pltpu.VMEM), out_shape),
        scratch_shapes=list(scratch),
        compiler_params=pltpu.CompilerParams(vmem_limit_bytes=40 * 2**20),
        cost_estimate=pl.CostEstimate(flops=flops, bytes_accessed=2**20, transcendentals=0),
        name=name,
    )


vmem = pl.BlockSpec(memory_space=pltpu.VMEM)
smem = pl.BlockSpec(memory_space=pltpu.SMEM)


def gram(left, right):
    return lax.dot_general(
        left, right, (((1,), (1,)), ((), ())), precision=precise, preferred_element_type=f32
    )


def parts_of(x):
    high = x.astype(bf16).astype(f32)
    return jnp.concatenate([high, x - high], axis=0).astype(bf16)


def whole_of(x16):
    half = x16.shape[0] // 2
    return x16[:half] + x16[half:]


def plain_dot(x, matrix):
    return lax.dot_general(x, matrix, (((1,), (0,)), ((), ())), preferred_element_type=f32)


def turned_dot(x, matrix):
    return lax.dot_general(x, matrix, (((1,), (1,)), ((), ())), preferred_element_type=f32)


def slot_of(cols, r, k, blocks):
    me = lax.axis_index("row")
    place = cols[r, k] - (me - 1) * blocks
    low = place < blocks
    high = place >= 2 * blocks
    swapped = jnp.where(low, place + 2 * blocks, jnp.where(high, place - 2 * blocks, place))
    return jnp.where(me % 2 == 0, swapped, place)


def prepare(loads, interior, stiff, r0, y0, dg, mk, *, blocks, shift):
    comps = loads.shape[1]
    bn = loads.shape[2] // blocks
    for b in range(blocks):
        nodes = pl.ds(b * bn, bn)
        inside = interior[:, nodes].astype(f32)
        inside = jnp.concatenate([inside] * comps, axis=1)
        field = jnp.concatenate([loads[:, c, nodes] for c in range(comps)], axis=1)
        own = jnp.concatenate([stiff[c : c + 1, nodes] for c in range(comps)], axis=1)
        r0[b] = field
        y0[b] = field * inside
        mk[b] = inside
        dg[b] = own - shift


def reverse_products(kh, kl, cols, ycat, acc):
    blocks, slots = kh.shape[0], kh.shape[1]
    acc[...] = jnp.zeros_like(acc)
    for r in range(blocks):
        for k in range(slots):
            s = slot_of(cols, r, k, blocks)
            acc[s] += plain_dot(ycat[r], kh[r, k]) + plain_dot(ycat[r], kl[r, k])


def reverse_first(coupling, cols, y0, kh, kl, out_e, out_m, out_o, acc):
    blocks, slots = coupling.shape[0], coupling.shape[1]
    acc[...] = jnp.zeros_like(acc)
    for r in range(blocks):
        ycat = parts_of(y0[r])
        for k in range(slots):
            matrix = coupling[r, k]
            high = matrix.astype(bf16)
            low = (matrix - high.astype(f32)).astype(bf16)
            kh[r, k] = high
            kl[r, k] = low
            s = slot_of(cols, r, k, blocks)
            acc[s] += plain_dot(ycat, high) + plain_dot(ycat, low)
    for b in range(blocks):
        out_e[b] = whole_of(acc[b])
        out_m[b] = whole_of(acc[blocks + b])
        out_o[b] = whole_of(acc[2 * blocks + b])


def forward(kh, kl, cols, y, y_e, y_o, x, dg, mk, own, result, xcat):
    blocks, slots = kh.shape[0], kh.shape[1]
    for b in range(blocks):
        xcat[b] = parts_of(y_e[b])
        xcat[blocks + b] = parts_of(y[b])
        xcat[2 * blocks + b] = parts_of(y_o[b])
    for r in range(blocks):
        total = jnp.zeros(xcat.shape[1:], f32)
        for k in range(slots):
            field = xcat[slot_of(cols, r, k, blocks)]
            total += turned_dot(field, kh[r, k]) + turned_dot(field, kl[r, k])
        result[r] = dg[r] * x[r] + mk[r] * (whole_of(total) + own[r])


def reverse_second(kh, kl, cols, y1, r0, w, dg, mk, out_e, out_m, out_o, grams, acc):
    blocks, slots = kh.shape[0], kh.shape[1]
    fields = y1.shape[1]
    acc[...] = jnp.zeros_like(acc)
    for r in range(blocks):
        ycat = parts_of(y1[r])
        for k in range(slots):
            s = slot_of(cols, r, k, blocks)
            acc[s] += plain_dot(ycat, kh[r, k]) + plain_dot(ycat, kl[r, k])
    h00 = h01 = h11 = h12 = jnp.zeros((fields, fields), f32)
    for b in range(blocks):
        own = whole_of(acc[blocks + b])
        out_e[b] = whole_of(acc[b])
        out_m[b] = own
        out_o[b] = whole_of(acc[2 * blocks + b])
        h00 += gram(r0[b], r0[b])
        h01 += gram(r0[b], w[b])
        h11 += gram(w[b], w[b])
        h12 += gram(w[b], dg[b] * w[b]) + gram(own, y1[b]) + gram(y1[b], own)
    rest = jnp.zeros((fields, grams.shape[1] - 4 * fields), f32)
    grams[...] = jnp.concatenate([h00, h01, h11, h12, rest], axis=1)


def halo_grams(out_e, out_o, y_e, y_o, grams, result):
    fields = out_e.shape[1]
    cross = jnp.zeros((fields, fields), f32)
    for b in range(out_e.shape[0]):
        cross += gram(out_e[b], y_e[b]) + gram(y_e[b], out_e[b])
        cross += gram(out_o[b], y_o[b]) + gram(y_o[b], out_o[b])
    before = jnp.zeros((fields, 3 * fields), f32)
    after = jnp.zeros((fields, result.shape[1] - 4 * fields), f32)
    result[...] = grams[...] + jnp.concatenate([before, cross, after], axis=1)


def eliminate(system, count):
    rows = lax.broadcasted_iota(jnp.int32, system.shape, 0)
    for k in range(count):
        pivot = system[k : k + 1, :] / system[k : k + 1, k : k + 1]
        rest = system - system[:, k : k + 1] * pivot
        system = jnp.where(rows == k, pivot, rest)
    return system


def small_dot(left, right):
    total = left[:, 0:1] * right[0:1, :]
    for k in range(1, left.shape[1]):
        total += left[:, k : k + 1] * right[k : k + 1, :]
    return total


def finish(*refs, rounds, shift):
    gram_refs = refs[:rounds]
    r0, w, up, mk, from_e, from_o, disp, resid = refs[rounds:]
    blocks, fields = r0.shape[0], r0.shape[1]
    comps = disp.shape[1]
    bn = disp.shape[2] // blocks
    sums = gram_refs[0][...]
    for ref in gram_refs[1:]:
        sums += ref[...]
    h00, h01, h11, h12 = (sums[:, i * fields : (i + 1) * fields] for i in range(4))
    eye = (
        lax.broadcasted_iota(jnp.int32, (fields, fields), 0)
        == lax.broadcasted_iota(jnp.int32, (fields, fields), 1)
    ).astype(f32)
    first = eliminate(jnp.concatenate([shift * h00 + h01, h00, h01], axis=1), fields)
    step, keep = first[:, fields : 2 * fields], first[:, 2 * fields : 3 * fields]
    inverse = eliminate(jnp.concatenate([h00, eye], axis=1), fields)[:, fields : 2 * fields]
    step_t = step.T
    keep_t = keep.T
    h00k = small_dot(h00, keep)
    h01k = small_dot(h01, keep)
    h01s = small_dot(h01, step)
    h11s = small_dot(h11, step)
    h12s = small_dot(h12, step)
    rho = small_dot(keep_t, h00k - h01s) + small_dot(step_t, h11s - h01k)
    mixing = small_dot(inverse, rho)
    lead = keep + mixing
    lead_t = lead.T
    h00p = small_dot(h00, lead)
    h01p = small_dot(h01, lead)
    h11p = small_dot(h11, lead)
    curvature = small_dot(lead_t, shift * (h00p - h01s) + h01p - h11s) + small_dot(
        step_t, shift * (h11s - h01p) + h12s - h11p
    )
    second = eliminate(jnp.concatenate([curvature, rho], axis=1), fields)
    after = second[:, fields : 2 * fields]
    lead_after = small_dot(lead, after)
    step_after = small_dot(step, after)
    zero = jnp.zeros_like(eye)
    mix = jnp.concatenate(
        [
            jnp.concatenate([step + lead_after, keep - shift * lead_after], axis=1),
            jnp.concatenate([-step_after, shift * step_after - step - lead_after], axis=1),
            jnp.concatenate([zero, step_after], axis=1),
        ],
        axis=0,
    )
    for b in range(blocks):
        u = up[b] + mk[b] * (from_e[b] + from_o[b])
        basis = jnp.concatenate([r0[b], w[b], u], axis=0)
        both = lax.dot_general(
            mix, basis, (((0,), (0,)), ((), ())), precision=precise, preferred_element_type=f32
        )
        for c in range(comps):
            piece = both[:, c * bn : (c + 1) * bn]
            disp[:, c, b * bn : (b + 1) * bn] = piece[:fields]
            resid[:, c, b * bn : (b + 1) * bn] = piece[fields:]


def even_swap(x):
    count = lax.axis_size("row")
    return lax.ppermute(x, "row", [(i, i ^ 1) for i in range(count)])


def odd_swap(x):
    groups, count = lax.axis_size("groups"), lax.axis_size("row")
    route = []
    for g in range(groups):
        for i in range(count):
            if i == 0 or i == count - 1:
                other = g ^ 1 if (g ^ 1) < groups else g
                route.append((g * count + i, other * count + i))
            else:
                route.append((g * count + i, g * count + ((i + 1) ^ 1) - 1))
    return lax.ppermute(x, ("groups", "row"), route)


def swapped_sums(x):
    count = lax.axis_size("row")
    base = 1
    while True:
        masks = [base, 2 * base, 3 * base] if 2 * base < count else [base]
        got = [
            lax.ppermute(x, "row", [(i, i ^ mask) for i in range(count)]) for mask in masks
        ]
        base *= len(masks) + 1
        if base >= count:
            return [x, *got]
        x = x + sum(got)


def shards(coupling, columns, stiff_diag, interior, loads):
    blocks, slots, width = coupling.shape[0], coupling.shape[1], coupling.shape[2]
    fields, comps, nodes = loads.shape
    shift = slot_shift * slots + diag_middle
    flops = 8 * 2 * fields * blocks * slots * width * width
    field = jax.ShapeDtypeStruct((blocks, fields, width), f32)
    row = jax.ShapeDtypeStruct((blocks, 1, width), f32)
    half = jax.ShapeDtypeStruct(coupling.shape, bf16)
    gram_shape = jax.ShapeDtypeStruct((fields, 128), f32)
    acc = pltpu.VMEM((3 * blocks, 2 * fields, width), f32)
    cat = pltpu.VMEM((3 * blocks, 2 * fields, width), bf16)

    r0, y0, dg, mk = call(
        lambda *refs: prepare(*refs, blocks=blocks, shift=diag_middle),
        (field, field, row, row), [vmem] * 3, name="prepare",
    )(loads, interior.reshape(1, nodes), stiff_diag)
    y0_e, y0_o = even_swap(y0), odd_swap(y0)
    kh, kl, a_e, a_m, a_o = call(
        reverse_first, (half, half, field, field, field), [vmem, smem, vmem],
        [acc], flops, name="reverse_first",
    )(coupling, columns, y0)
    b_e, b_o = even_swap(a_e), odd_swap(a_o)
    wp = call(
        forward, field, [vmem, vmem, smem] + [vmem] * 7, [cat], flops, name="forward_first",
    )(kh, kl, columns, y0, y0_e, y0_o, r0, dg, mk, a_m)
    w = wp + mk * (b_e + b_o)
    y1 = w * mk
    y1_e, y1_o = even_swap(y1), odd_swap(y1)
    c_e, c_m, c_o, grams = call(
        reverse_second, (field, field, field, gram_shape), [vmem, vmem, smem] + [vmem] * 5,
        [acc], flops, name="reverse_second",
    )(kh, kl, columns, y1, r0, w, dg, mk)
    grams = call(halo_grams, gram_shape, [vmem] * 5, name="halo_grams")(
        c_e, c_o, y1_e, y1_o, grams
    )
    sums = swapped_sums(grams)
    d_e, d_o = even_swap(c_e), odd_swap(c_o)
    up = call(
        forward, field, [vmem, vmem, smem] + [vmem] * 7, [cat], flops, name="forward_second",
    )(kh, kl, columns, y1, y1_e, y1_o, w, dg, mk, c_m)
    out = jax.ShapeDtypeStruct(loads.shape, f32)
    return call(
        lambda *refs: finish(*refs, rounds=len(sums), shift=shift),
        (out, out), [vmem] * (len(sums) + 6), name="finish",
    )(*sums, r0, w, up, mk, d_e, d_o)


def solution(mesh):
    placed = (
        P(("groups", "row"), None, None, None),
        P(("groups", "row"), None),
        P(None, ("groups", "row")),
        P(("groups", "row")),
        P(None, None, ("groups", "row")),
    )
    return jax.shard_map(
        shards,
        mesh=mesh,
        in_specs=placed,
        out_specs=(P(None, None, ("groups", "row")), P(None, None, ("groups", "row"))),
        check_vma=False,
    )
```

```python
import jax
import jax.numpy as jnp
from jax import lax
from jax.experimental import pallas as pl
from jax.experimental.pallas import tpu as pltpu
from jax.sharding import PartitionSpec as P

f32 = jnp.float32
bf16 = jnp.bfloat16
precise = lax.Precision.HIGHEST
slot_shift = 1.2
diag_middle = 1.25


def call(body, out_shape, in_specs, scratch=(), flops=0, name=None, limit=24):
    return pl.pallas_call(
        body,
        out_shape=out_shape,
        in_specs=in_specs,
        out_specs=jax.tree.map(lambda _: pl.BlockSpec(memory_space=pltpu.VMEM), out_shape),
        scratch_shapes=list(scratch),
        compiler_params=pltpu.CompilerParams(vmem_limit_bytes=limit * 2**20),
        cost_estimate=pl.CostEstimate(flops=flops, bytes_accessed=2**20, transcendentals=0),
        name=name,
    )


vmem = pl.BlockSpec(memory_space=pltpu.VMEM)
smem = pl.BlockSpec(memory_space=pltpu.SMEM)


def in_hbm(x):
    return pltpu.with_memory_space_constraint(x, pltpu.HBM)


def gram(left, right):
    return lax.dot_general(
        left, right, (((1,), (1,)), ((), ())), precision=precise, preferred_element_type=f32
    )


def parts_of(x):
    high = x.astype(bf16).astype(f32)
    return jnp.concatenate([high, x - high], axis=0).astype(bf16)


def whole_of(x16):
    half = x16.shape[0] // 2
    return x16[:half] + x16[half:]


def plain_dot(x, matrix):
    return lax.dot_general(x, matrix, (((1,), (0,)), ((), ())), preferred_element_type=f32)


def turned_dot(x, matrix):
    return lax.dot_general(x, matrix, (((1,), (1,)), ((), ())), preferred_element_type=f32)


def slot_of(cols, r, k, blocks):
    me = lax.axis_index("row")
    place = cols[r, k] - (me - 1) * blocks
    low = place < blocks
    high = place >= 2 * blocks
    swapped = jnp.where(low, place + 2 * blocks, jnp.where(high, place - 2 * blocks, place))
    return jnp.where(me % 2 == 0, swapped, place)


def prepare(
    loads_in, interior_in, stiff_in, r0, y0, dg, mk, loads, interior, stiff, sems, *, blocks, shift
):
    comps = loads.shape[0]
    bn = loads.shape[2] // blocks
    fetches = [
        pltpu.make_async_copy(source, target, sems.at[i])
        for i, (source, target) in enumerate(
            ((loads_in, loads), (interior_in, interior), (stiff_in, stiff))
        )
    ]
    for fetch in fetches:
        fetch.start()
    for fetch in fetches:
        fetch.wait()
    inside_all = interior[...].astype(f32).reshape(1, -1)
    for b in range(blocks):
        nodes = pl.ds(b * bn, bn)
        inside = inside_all[:, b * bn : (b + 1) * bn]
        inside = jnp.concatenate([inside] * comps, axis=1)
        field = jnp.concatenate([loads[c, :, nodes] for c in range(comps)], axis=1)
        own = jnp.concatenate([stiff[c : c + 1, nodes] for c in range(comps)], axis=1)
        r0[b] = field
        y0[b] = field * inside
        mk[b] = inside
        dg[b] = own - shift


def reverse_products(kh, kl, cols, ycat, acc):
    blocks, slots = kh.shape[0], kh.shape[1]
    acc[...] = jnp.zeros_like(acc)
    for r in range(blocks):
        for k in range(slots):
            s = slot_of(cols, r, k, blocks)
            acc[s] += plain_dot(ycat[r], kh[r, k]) + plain_dot(ycat[r], kl[r, k])


def reverse_first(coupling, cols, y0, kh, kl, out_e, out_m, out_o, acc):
    blocks, slots = coupling.shape[0], coupling.shape[1]
    acc[...] = jnp.zeros_like(acc)
    for r in range(blocks):
        ycat = parts_of(y0[r])
        for k in range(slots):
            matrix = coupling[r, k]
            high = matrix.astype(bf16)
            low = (matrix - high.astype(f32)).astype(bf16)
            kh[r, k] = high
            kl[r, k] = low
            s = slot_of(cols, r, k, blocks)
            acc[s] += plain_dot(ycat, high) + plain_dot(ycat, low)
    for b in range(blocks):
        out_e[b] = whole_of(acc[b])
        out_m[b] = whole_of(acc[blocks + b])
        out_o[b] = whole_of(acc[2 * blocks + b])


def forward(kh, kl, cols, y, y_e, y_o, x, dg, mk, own, result, xcat):
    blocks, slots = kh.shape[0], kh.shape[1]
    for b in range(blocks):
        xcat[b] = parts_of(y_e[b])
        xcat[blocks + b] = parts_of(y[b])
        xcat[2 * blocks + b] = parts_of(y_o[b])
    for r in range(blocks):
        total = jnp.zeros(xcat.shape[1:], f32)
        for k in range(slots):
            field = xcat[slot_of(cols, r, k, blocks)]
            total += turned_dot(field, kh[r, k]) + turned_dot(field, kl[r, k])
        result[r] = dg[r] * x[r] + mk[r] * (whole_of(total) + own[r])


def reverse_second(kh, kl, cols, y1, r0, w, dg, mk, out_e, out_m, out_o, grams, acc):
    blocks, slots = kh.shape[0], kh.shape[1]
    fields = y1.shape[1]
    acc[...] = jnp.zeros_like(acc)
    for r in range(blocks):
        ycat = parts_of(y1[r])
        for k in range(slots):
            s = slot_of(cols, r, k, blocks)
            acc[s] += plain_dot(ycat, kh[r, k]) + plain_dot(ycat, kl[r, k])
    h00 = h01 = h11 = h12 = jnp.zeros((fields, fields), f32)
    for b in range(blocks):
        own = whole_of(acc[blocks + b])
        out_e[b] = whole_of(acc[b])
        out_m[b] = own
        out_o[b] = whole_of(acc[2 * blocks + b])
        h00 += gram(r0[b], r0[b])
        h01 += gram(r0[b], w[b])
        h11 += gram(w[b], w[b])
        h12 += gram(w[b], dg[b] * w[b]) + gram(own, y1[b]) + gram(y1[b], own)
    rest = jnp.zeros((fields, grams.shape[1] - 4 * fields), f32)
    grams[...] = jnp.concatenate([h00, h01, h11, h12, rest], axis=1)


def halo_grams(out_e, out_o, y_e, y_o, grams, result):
    fields = out_e.shape[1]
    cross = jnp.zeros((fields, fields), f32)
    for b in range(out_e.shape[0]):
        cross += gram(out_e[b], y_e[b]) + gram(y_e[b], out_e[b])
        cross += gram(out_o[b], y_o[b]) + gram(y_o[b], out_o[b])
    before = jnp.zeros((fields, 3 * fields), f32)
    after = jnp.zeros((fields, result.shape[1] - 4 * fields), f32)
    result[...] = grams[...] + jnp.concatenate([before, cross, after], axis=1)


def eliminate(system, count):
    rows = lax.broadcasted_iota(jnp.int32, system.shape, 0)
    for k in range(count):
        pivot = system[k : k + 1, :] / system[k : k + 1, k : k + 1]
        rest = system - system[:, k : k + 1] * pivot
        system = jnp.where(rows == k, pivot, rest)
    return system


def small_dot(left, right):
    total = left[:, 0:1] * right[0:1, :]
    for k in range(1, left.shape[1]):
        total += left[:, k : k + 1] * right[k : k + 1, :]
    return total


def finish(*refs, rounds, shift):
    gram_refs = refs[:rounds]
    r0, w, up, mk, from_e, from_o, disp, resid = refs[rounds:]
    blocks, fields = r0.shape[0], r0.shape[1]
    comps = disp.shape[0]
    bn = disp.shape[2] // blocks
    sums = gram_refs[0][...]
    for ref in gram_refs[1:]:
        sums += ref[...]
    h00, h01, h11, h12 = (sums[:, i * fields : (i + 1) * fields] for i in range(4))
    eye = (
        lax.broadcasted_iota(jnp.int32, (fields, fields), 0)
        == lax.broadcasted_iota(jnp.int32, (fields, fields), 1)
    ).astype(f32)
    first = eliminate(jnp.concatenate([shift * h00 + h01, h00, h01], axis=1), fields)
    step, keep = first[:, fields : 2 * fields], first[:, 2 * fields : 3 * fields]
    inverse = eliminate(jnp.concatenate([h00, eye], axis=1), fields)[:, fields : 2 * fields]
    step_t = step.T
    keep_t = keep.T
    h00k = small_dot(h00, keep)
    h01k = small_dot(h01, keep)
    h01s = small_dot(h01, step)
    h11s = small_dot(h11, step)
    h12s = small_dot(h12, step)
    rho = small_dot(keep_t, h00k - h01s) + small_dot(step_t, h11s - h01k)
    mixing = small_dot(inverse, rho)
    lead = keep + mixing
    lead_t = lead.T
    h00p = small_dot(h00, lead)
    h01p = small_dot(h01, lead)
    h11p = small_dot(h11, lead)
    curvature = small_dot(lead_t, shift * (h00p - h01s) + h01p - h11s) + small_dot(
        step_t, shift * (h11s - h01p) + h12s - h11p
    )
    second = eliminate(jnp.concatenate([curvature, rho], axis=1), fields)
    after = second[:, fields : 2 * fields]
    lead_after = small_dot(lead, after)
    step_after = small_dot(step, after)
    zero = jnp.zeros_like(eye)
    mix = jnp.concatenate(
        [
            jnp.concatenate([step + lead_after, keep - shift * lead_after], axis=1),
            jnp.concatenate([-step_after, shift * step_after - step - lead_after], axis=1),
            jnp.concatenate([zero, step_after], axis=1),
        ],
        axis=0,
    )
    for b in range(blocks):
        u = up[b] + mk[b] * (from_e[b] + from_o[b])
        basis = jnp.concatenate([r0[b], w[b], u], axis=0)
        both = lax.dot_general(
            mix, basis, (((0,), (0,)), ((), ())), precision=precise, preferred_element_type=f32
        )
        for c in range(comps):
            piece = both[:, c * bn : (c + 1) * bn]
            disp[c, :, b * bn : (b + 1) * bn] = piece[:fields]
            resid[c, :, b * bn : (b + 1) * bn] = piece[fields:]


def even_swap(x):
    count = lax.axis_size("row")
    return lax.ppermute(x, "row", [(i, i ^ 1) for i in range(count)])


def odd_swap(x):
    groups, count = lax.axis_size("groups"), lax.axis_size("row")
    route = []
    for g in range(groups):
        for i in range(count):
            if i == 0 or i == count - 1:
                other = g ^ 1 if (g ^ 1) < groups else g
                route.append((g * count + i, other * count + i))
            else:
                route.append((g * count + i, g * count + ((i + 1) ^ 1) - 1))
    return lax.ppermute(x, ("groups", "row"), route)


def swapped_sums(x):
    count = lax.axis_size("row")
    base = 1
    while True:
        masks = [base, 2 * base, 3 * base] if 2 * base < count else [base]
        got = [
            lax.ppermute(x, "row", [(i, i ^ mask) for i in range(count)]) for mask in masks
        ]
        base *= len(masks) + 1
        if base >= count:
            return [x, *got]
        x = x + sum(got)


def shards(coupling, columns, stiff_diag, interior, loads):
    blocks, slots, width = coupling.shape[0], coupling.shape[1], coupling.shape[2]
    fields, comps, nodes = loads.shape
    shift = slot_shift * slots + diag_middle
    flops = 8 * 2 * fields * blocks * slots * width * width
    field = jax.ShapeDtypeStruct((blocks, fields, width), f32)
    row = jax.ShapeDtypeStruct((blocks, 1, width), f32)
    half = jax.ShapeDtypeStruct(coupling.shape, bf16)
    gram_shape = jax.ShapeDtypeStruct((fields, 128), f32)
    acc = pltpu.VMEM((3 * blocks, 2 * fields, width), f32)
    cat = pltpu.VMEM((3 * blocks, 2 * fields, width), bf16)

    r0, y0, dg, mk = call(
        lambda *refs: prepare(*refs, blocks=blocks, shift=diag_middle),
        (field, field, row, row), [pl.BlockSpec(memory_space=pl.ANY)] * 3,
        [
            pltpu.VMEM((comps, fields, nodes), f32),
            pltpu.VMEM((nodes,), jnp.int32),
            pltpu.VMEM((comps, nodes), f32),
            pltpu.SemaphoreType.DMA((3,)),
        ],
        flops=10**10,
        name="prepare",
    )(*(in_hbm(x) for x in (loads.transpose(1, 0, 2), interior, stiff_diag)))
    y0_e, y0_o = even_swap(y0), odd_swap(y0)
    kh, kl, a_e, a_m, a_o = call(
        reverse_first, (half, half, field, field, field), [vmem, smem, vmem],
        [acc], flops, name="reverse_first",
    )(coupling, columns, y0)
    b_e, b_o = even_swap(a_e), odd_swap(a_o)
    wp = call(
        forward, field, [vmem, vmem, smem] + [vmem] * 7, [cat], flops, name="forward_first",
    )(kh, kl, columns, y0, y0_e, y0_o, r0, dg, mk, a_m)
    w = wp + mk * (b_e + b_o)
    y1 = w * mk
    y1_e, y1_o = even_swap(y1), odd_swap(y1)
    c_e, c_m, c_o, grams = call(
        reverse_second, (field, field, field, gram_shape), [vmem, vmem, smem] + [vmem] * 5,
        [acc], flops, name="reverse_second",
    )(kh, kl, columns, y1, r0, w, dg, mk)
    grams = call(halo_grams, gram_shape, [vmem] * 5, name="halo_grams")(
        c_e, c_o, y1_e, y1_o, grams
    )
    sums = swapped_sums(grams)
    d_e, d_o = even_swap(c_e), odd_swap(c_o)
    up = call(
        forward, field, [vmem, vmem, smem] + [vmem] * 7, [cat], flops, name="forward_second",
    )(kh, kl, columns, y1, y1_e, y1_o, w, dg, mk, c_m)
    out = jax.ShapeDtypeStruct((comps, fields, nodes), f32)
    disp, resid = call(
        lambda *refs: finish(*refs, rounds=len(sums), shift=shift),
        (out, out), [vmem] * (len(sums) + 6), name="finish",
    )(*sums, r0, w, up, mk, d_e, d_o)
    return disp.transpose(1, 0, 2), resid.transpose(1, 0, 2)


def solution(mesh):
    placed = (
        P(("groups", "row"), None, None, None),
        P(("groups", "row"), None),
        P(None, ("groups", "row")),
        P(("groups", "row")),
        P(None, None, ("groups", "row")),
    )
    return jax.shard_map(
        shards,
        mesh=mesh,
        in_specs=placed,
        out_specs=(P(None, None, ("groups", "row")), P(None, None, ("groups", "row"))),
        check_vma=False,
    )
```

```python
import jax
import jax.numpy as jnp
from jax import lax
from jax.experimental import pallas as pl
from jax.experimental.pallas import tpu as pltpu
from jax.sharding import PartitionSpec as P

f32 = jnp.float32
bf16 = jnp.bfloat16
slot_shift = 1.2
diag_middle = 1.25


def call(body, out_shape, in_specs, scratch=(), flops=0, name=None, limit=24):
    return pl.pallas_call(
        body,
        out_shape=out_shape,
        in_specs=in_specs,
        out_specs=jax.tree.map(lambda _: pl.BlockSpec(memory_space=pltpu.VMEM), out_shape),
        scratch_shapes=list(scratch),
        compiler_params=pltpu.CompilerParams(vmem_limit_bytes=limit * 2**20),
        cost_estimate=pl.CostEstimate(flops=flops, bytes_accessed=2**20, transcendentals=0),
        name=name,
    )


vmem = pl.BlockSpec(memory_space=pltpu.VMEM)
smem = pl.BlockSpec(memory_space=pltpu.SMEM)


def in_hbm(x):
    return pltpu.with_memory_space_constraint(x, pltpu.HBM)


def thirds_of(x):
    high = x.astype(bf16).astype(f32)
    rest = x - high
    middle = rest.astype(bf16).astype(f32)
    return jnp.concatenate([high, middle, rest - middle], axis=0).astype(bf16)


def gram(left, right):
    a, b = left.shape[0], right.shape[0]
    parts = turned_dot(thirds_of(left), thirds_of(right))
    rows = parts[:a] + (parts[a : 2 * a] + parts[2 * a :])
    return rows[:, :b] + (rows[:, b : 2 * b] + rows[:, 2 * b :])


def parts_of(x):
    high = x.astype(bf16).astype(f32)
    return jnp.concatenate([high, x - high], axis=0).astype(bf16)


def whole_of(x16):
    half = x16.shape[0] // 2
    return x16[:half] + x16[half:]


def plain_dot(x, matrix):
    return lax.dot_general(x, matrix, (((1,), (0,)), ((), ())), preferred_element_type=f32)


def turned_dot(x, matrix):
    return lax.dot_general(x, matrix, (((1,), (1,)), ((), ())), preferred_element_type=f32)


def slot_of(cols, r, k, blocks):
    me = lax.axis_index("row")
    place = cols[r, k] - (me - 1) * blocks
    low = place < blocks
    high = place >= 2 * blocks
    swapped = jnp.where(low, place + 2 * blocks, jnp.where(high, place - 2 * blocks, place))
    return jnp.where(me % 2 == 0, swapped, place)


def prepare(
    loads_in, interior_in, stiff_in, r0, y0, dg, mk, loads, interior, stiff, sems, *, blocks, shift
):
    comps = loads.shape[0]
    bn = loads.shape[2] // blocks
    fetches = [
        pltpu.make_async_copy(source, target, sems.at[i])
        for i, (source, target) in enumerate(
            ((loads_in, loads), (interior_in, interior), (stiff_in, stiff))
        )
    ]
    for fetch in fetches:
        fetch.start()
    for fetch in fetches:
        fetch.wait()
    inside_all = interior[...].astype(f32).reshape(1, -1)
    for b in range(blocks):
        nodes = pl.ds(b * bn, bn)
        inside = inside_all[:, b * bn : (b + 1) * bn]
        inside = jnp.concatenate([inside] * comps, axis=1)
        field = jnp.concatenate([loads[c, :, nodes] for c in range(comps)], axis=1)
        own = jnp.concatenate([stiff[c : c + 1, nodes] for c in range(comps)], axis=1)
        r0[b] = field
        y0[b] = field * inside
        mk[b] = inside
        dg[b] = own - shift


def reverse_products(kh, kl, cols, ycat, acc):
    blocks, slots = kh.shape[0], kh.shape[1]
    acc[...] = jnp.zeros_like(acc)
    for r in range(blocks):
        for k in range(slots):
            s = slot_of(cols, r, k, blocks)
            acc[s] += plain_dot(ycat[r], kh[r, k]) + plain_dot(ycat[r], kl[r, k])


def reverse_first(coupling, cols, y0, kh, kl, out_e, out_m, out_o, acc):
    blocks, slots = coupling.shape[0], coupling.shape[1]
    acc[...] = jnp.zeros_like(acc)
    for r in range(blocks):
        ycat = parts_of(y0[r])
        for k in range(slots):
            matrix = coupling[r, k]
            high = matrix.astype(bf16)
            low = (matrix - high.astype(f32)).astype(bf16)
            kh[r, k] = high
            kl[r, k] = low
            s = slot_of(cols, r, k, blocks)
            acc[s] += plain_dot(ycat, high) + plain_dot(ycat, low)
    for b in range(blocks):
        out_e[b] = whole_of(acc[b])
        out_m[b] = whole_of(acc[blocks + b])
        out_o[b] = whole_of(acc[2 * blocks + b])


def forward(kh, kl, cols, y, y_e, y_o, x, dg, mk, *rest):
    *reverse, result, xcat = rest
    blocks, slots = kh.shape[0], kh.shape[1]
    for b in range(blocks):
        xcat[b] = parts_of(y_e[b])
        xcat[blocks + b] = parts_of(y[b])
        xcat[2 * blocks + b] = parts_of(y_o[b])
    for r in range(blocks):
        total = jnp.zeros(xcat.shape[1:], f32)
        for k in range(slots):
            field = xcat[slot_of(cols, r, k, blocks)]
            total += turned_dot(field, kh[r, k]) + turned_dot(field, kl[r, k])
        summed = whole_of(total)
        for part in reverse:
            summed += part[r]
        result[r] = dg[r] * x[r] + mk[r] * summed


def reverse_second(kh, kl, cols, y1, r0, w, dg, mk, out_e, out_m, out_o, grams, acc):
    blocks, slots = kh.shape[0], kh.shape[1]
    n = y1.shape[1]
    acc[...] = jnp.zeros_like(acc)
    for r in range(blocks):
        ycat = parts_of(y1[r])
        for k in range(slots):
            s = slot_of(cols, r, k, blocks)
            acc[s] += plain_dot(ycat, kh[r, k]) + plain_dot(ycat, kl[r, k])
    total = jnp.zeros((3 * n, 4 * n), f32)
    for b in range(blocks):
        own = whole_of(acc[blocks + b])
        out_e[b] = whole_of(acc[b])
        out_m[b] = own
        out_o[b] = whole_of(acc[2 * blocks + b])
        free = mk[b] * own
        total += gram(
            jnp.concatenate([r0[b], w[b], free], axis=0),
            jnp.concatenate([r0[b], w[b], dg[b] * w[b], free], axis=0),
        )
    h12 = total[n : 2 * n, 2 * n : 3 * n] + total[n : 2 * n, 3 * n :] + total[2 * n :, n : 2 * n]
    rest = jnp.zeros((n, grams.shape[1] - 4 * n), f32)
    grams[...] = jnp.concatenate(
        [total[:n, : 2 * n], total[n : 2 * n, n : 2 * n], h12, rest], axis=1
    )


def halo_grams(out_e, out_o, y_e, y_o, grams, result):
    n = out_e.shape[1]
    total = jnp.zeros((2 * n, 2 * n), f32)
    for b in range(out_e.shape[0]):
        for out, y in ((out_e, y_e), (out_o, y_o)):
            total += gram(
                jnp.concatenate([out[b], y[b]], axis=0), jnp.concatenate([y[b], out[b]], axis=0)
            )
    cross = total[:n, :n] + total[n:, n:]
    before = jnp.zeros((n, 3 * n), f32)
    after = jnp.zeros((n, result.shape[1] - 4 * n), f32)
    result[...] = grams[...] + jnp.concatenate([before, cross, after], axis=1)


def eliminate(systems):
    count = systems[0][0].shape[0]
    rows = lax.broadcasted_iota(jnp.int32, (count, 128), 0)
    spread = [
        [jnp.broadcast_to(matrix[:, k : k + 1], (count, 128)) for k in range(count)]
        for matrix, _ in systems
    ]
    sides = [side for _, side in systems]
    for k in range(count):
        for i, columns in enumerate(spread):
            column = columns[k]
            scale = 1.0 / column[k : k + 1]

            def step(x):
                width = x.shape[1]
                pivot = x[k : k + 1] * scale[:, :width]
                return jnp.where(rows[:, :width] == k, pivot, x - column[:, :width] * pivot)

            spread[i] = [step(c) if j > k else c for j, c in enumerate(columns)]
            sides[i] = step(sides[i])
    return sides


def columns_of(matrix):
    return [matrix[:, k : k + 1] for k in range(matrix.shape[1])]


def small_dot(columns, right):
    terms = [column * right[k : k + 1, :] for k, column in enumerate(columns)]
    while len(terms) > 1:
        terms = [a + b for a, b in zip(terms[::2], terms[1::2])]
    return terms[0]


def finish(*refs, rounds, shift):
    gram_refs = refs[:rounds]
    r0, w, u, disp, resid = refs[rounds:]
    blocks, n = r0.shape[0], r0.shape[1]
    comps = disp.shape[0]
    bn = disp.shape[2] // blocks
    sums = gram_refs[0][...]
    for ref in gram_refs[1:]:
        sums += ref[...]
    h00, h01, h11, h12 = (sums[:, i * n : (i + 1) * n] for i in range(4))
    eye = (
        lax.broadcasted_iota(jnp.int32, (n, n), 0) == lax.broadcasted_iota(jnp.int32, (n, n), 1)
    ).astype(f32)
    first, inverse0 = eliminate(
        [(shift * h00 + h01, jnp.concatenate([h00, h01, eye], axis=1)), (h00, eye)]
    )
    step, keep, inverse = (first[:, i * n : (i + 1) * n] for i in range(3))
    c00, c01, c11, c12 = (columns_of(h) for h in (h00, h01, h11, h12))
    step_t, keep_t = small_dot(c00, inverse), small_dot(c01, inverse)
    h11s = small_dot(c11, step)
    past = h11s - small_dot(c01, keep)
    image = small_dot(c12, step) + shift * past - small_dot(c11, keep)
    both = small_dot(
        columns_of(step_t), jnp.concatenate([past, image, h11 + shift * h01], axis=1)
    )
    rho = both[:, :n]
    mixing = small_dot(columns_of(inverse0), rho)
    curvature = both[:, n : 2 * n] - small_dot(columns_of(both[:, 2 * n :]), mixing)
    rho_columns = columns_of(rho)
    lead_t = keep_t + small_dot(rho_columns, inverse0)
    after_t = small_dot(rho_columns, eliminate([(curvature, eye)])[0])
    moved = small_dot(columns_of(after_t), jnp.concatenate([lead_t, step_t], axis=1))
    lead_after, step_after = moved[:, :n], moved[:, n:]
    for_disp = (step_t + lead_after, -step_after)
    for_resid = (
        keep_t - shift * lead_after, shift * step_after - step_t - lead_after, step_after
    )
    for mix, out in ((for_disp, disp), (for_resid, resid)):
        mix_columns = [columns_of(m) for m in mix]
        for b in range(blocks):
            total = None
            for columns, x in zip(mix_columns, (r0, w, u)):
                for g in range(n):
                    term = columns[g] * x[b, g : g + 1, :]
                    total = term if total is None else total + term
            for c in range(comps):
                out[c, :, b * bn : (b + 1) * bn] = total[:, c * bn : (c + 1) * bn]


def even_swap(x):
    count = lax.axis_size("row")
    return lax.ppermute(x, "row", [(i, i ^ 1) for i in range(count)])


def odd_swap(x):
    groups, count = lax.axis_size("groups"), lax.axis_size("row")
    route = []
    for g in range(groups):
        for i in range(count):
            if i == 0 or i == count - 1:
                other = g ^ 1 if (g ^ 1) < groups else g
                route.append((g * count + i, other * count + i))
            else:
                route.append((g * count + i, g * count + ((i + 1) ^ 1) - 1))
    return lax.ppermute(x, ("groups", "row"), route)


def swapped_sums(x):
    count = lax.axis_size("row")
    base = 1
    while True:
        masks = [base, 2 * base, 3 * base] if 2 * base < count else [base]
        got = [
            lax.ppermute(x, "row", [(i, i ^ mask) for i in range(count)]) for mask in masks
        ]
        base *= len(masks) + 1
        if base >= count:
            return [x, *got]
        x = x + sum(got)


def shards(coupling, columns, stiff_diag, interior, loads):
    blocks, slots, width = coupling.shape[0], coupling.shape[1], coupling.shape[2]
    fields, comps, nodes = loads.shape
    shift = slot_shift * slots + diag_middle
    flops = 8 * 2 * fields * blocks * slots * width * width
    field = jax.ShapeDtypeStruct((blocks, fields, width), f32)
    row = jax.ShapeDtypeStruct((blocks, 1, width), f32)
    half = jax.ShapeDtypeStruct(coupling.shape, bf16)
    gram_shape = jax.ShapeDtypeStruct((fields, 128), f32)
    acc = pltpu.VMEM((3 * blocks, 2 * fields, width), f32)
    cat = pltpu.VMEM((3 * blocks, 2 * fields, width), bf16)

    r0, y0, dg, mk = call(
        lambda *refs: prepare(*refs, blocks=blocks, shift=diag_middle),
        (field, field, row, row), [pl.BlockSpec(memory_space=pl.ANY)] * 3,
        [
            pltpu.VMEM((comps, fields, nodes), f32),
            pltpu.VMEM((nodes,), jnp.int32),
            pltpu.VMEM((comps, nodes), f32),
            pltpu.SemaphoreType.DMA((3,)),
        ],
        flops=10**10,
        name="prepare",
    )(*(in_hbm(x) for x in (loads.transpose(1, 0, 2), interior, stiff_diag)))
    y0_e, y0_o = even_swap(y0), odd_swap(y0)
    kh, kl, a_e, a_m, a_o = call(
        reverse_first, (half, half, field, field, field), [vmem, smem, vmem],
        [acc], flops, name="reverse_first",
    )(coupling, columns, y0)
    b_e, b_o = even_swap(a_e), odd_swap(a_o)
    wp = call(
        forward, field, [vmem, vmem, smem] + [vmem] * 7, [cat], flops, name="forward_first",
    )(kh, kl, columns, y0, y0_e, y0_o, r0, dg, mk, a_m)
    w = wp + mk * (b_e + b_o)
    y1 = w * mk
    y1_e, y1_o = even_swap(y1), odd_swap(y1)
    c_e, c_m, c_o, grams = call(
        reverse_second, (field, field, field, gram_shape), [vmem, vmem, smem] + [vmem] * 5,
        [acc], flops, name="reverse_second",
    )(kh, kl, columns, y1, r0, w, dg, mk)
    grams = call(halo_grams, gram_shape, [vmem] * 5, name="halo_grams")(
        c_e, c_o, y1_e, y1_o, grams
    )
    sums = swapped_sums(grams)
    d_e, d_o = even_swap(c_e), odd_swap(c_o)
    u = call(
        forward, field, [vmem, vmem, smem] + [vmem] * 9, [cat], flops, name="forward_second",
    )(kh, kl, columns, y1, y1_e, y1_o, w, dg, mk, c_m, d_e, d_o)
    out = jax.ShapeDtypeStruct((comps, fields, nodes), f32)
    disp, resid = call(
        lambda *refs: finish(*refs, rounds=len(sums), shift=shift),
        (out, out), [vmem] * (len(sums) + 3), name="finish",
    )(*sums, r0, w, u)
    return disp.transpose(1, 0, 2), resid.transpose(1, 0, 2)


def solution(mesh):
    placed = (
        P(("groups", "row"), None, None, None),
        P(("groups", "row"), None),
        P(None, ("groups", "row")),
        P(("groups", "row")),
        P(None, None, ("groups", "row")),
    )
    return jax.shard_map(
        shards,
        mesh=mesh,
        in_specs=placed,
        out_specs=(P(None, None, ("groups", "row")), P(None, None, ("groups", "row"))),
        check_vma=False,
    )
```

```python
import functools

import jax
import jax.numpy as jnp
from jax import lax
from jax.experimental import pallas as pl
from jax.experimental.pallas import tpu as pltpu
from jax.sharding import PartitionSpec as P

f32 = jnp.float32
bf16 = jnp.bfloat16
slot_shift = 1.2
diag_middle = 1.25


def call(body, out_shape, in_specs, scratch=(), flops=0, name=None, limit=24):
    return pl.pallas_call(
        body,
        out_shape=out_shape,
        in_specs=in_specs,
        out_specs=jax.tree.map(lambda _: pl.BlockSpec(memory_space=pltpu.VMEM), out_shape),
        scratch_shapes=list(scratch),
        compiler_params=pltpu.CompilerParams(vmem_limit_bytes=limit * 2**20),
        cost_estimate=pl.CostEstimate(flops=flops, bytes_accessed=2**20, transcendentals=0),
        name=name,
    )


vmem = pl.BlockSpec(memory_space=pltpu.VMEM)
smem = pl.BlockSpec(memory_space=pltpu.SMEM)


def in_hbm(x):
    return pltpu.with_memory_space_constraint(x, pltpu.HBM)


def thirds_of(x):
    high = x.astype(bf16).astype(f32)
    rest = x - high
    middle = rest.astype(bf16).astype(f32)
    return jnp.concatenate([high, middle, rest - middle], axis=0).astype(bf16)


def gram(left, right):
    a, b = left.shape[0], right.shape[0]
    parts = turned_dot(thirds_of(left), thirds_of(right))
    rows = parts[:a] + (parts[a : 2 * a] + parts[2 * a :])
    return rows[:, :b] + (rows[:, b : 2 * b] + rows[:, 2 * b :])


def parts_of(x):
    high = x.astype(bf16).astype(f32)
    return jnp.concatenate([high, x - high], axis=0).astype(bf16)


def whole_of(x16):
    half = x16.shape[0] // 2
    return x16[:half] + x16[half:]


def plain_dot(x, matrix):
    return lax.dot_general(x, matrix, (((1,), (0,)), ((), ())), preferred_element_type=f32)


def turned_dot(x, matrix):
    return lax.dot_general(x, matrix, (((1,), (1,)), ((), ())), preferred_element_type=f32)


def slot_of(cols, r, k, blocks):
    me = lax.axis_index("row")
    place = cols[r, k] - (me - 1) * blocks
    low = place < blocks
    high = place >= 2 * blocks
    swapped = jnp.where(low, place + 2 * blocks, jnp.where(high, place - 2 * blocks, place))
    return jnp.where(me % 2 == 0, swapped, place)


def prepare(
    loads_in, interior_in, stiff_in, r0, y0, dg, mk, loads, interior, stiff, sems, *, blocks, shift
):
    comps = loads.shape[0]
    bn = loads.shape[2] // blocks
    fetches = [
        pltpu.make_async_copy(source, target, sems.at[i])
        for i, (source, target) in enumerate(
            ((loads_in, loads), (interior_in, interior), (stiff_in, stiff))
        )
    ]
    for fetch in fetches:
        fetch.start()
    for fetch in fetches:
        fetch.wait()
    inside_all = interior[...].astype(f32).reshape(1, -1)
    for b in range(blocks):
        nodes = pl.ds(b * bn, bn)
        inside = inside_all[:, b * bn : (b + 1) * bn]
        inside = jnp.concatenate([inside] * comps, axis=1)
        field = jnp.concatenate([loads[c, :, nodes] for c in range(comps)], axis=1)
        own = jnp.concatenate([stiff[c : c + 1, nodes] for c in range(comps)], axis=1)
        r0[b] = field
        y0[b] = field * inside
        mk[b] = inside
        dg[b] = own - shift


def reverse_first(coupling, cols, y0, kh, kl, th, out_e, out_m, out_o, acc):
    blocks, slots = coupling.shape[0], coupling.shape[1]
    acc[...] = jnp.zeros_like(acc)
    for r in range(blocks):
        ycat = parts_of(y0[r])
        for k in range(slots):
            matrix = coupling[r, k]
            high = matrix.astype(bf16)
            low = (matrix - high.astype(f32)).astype(bf16)
            kh[r, k] = high
            kl[r, k] = low
            th[r, k] = high.T
            s = slot_of(cols, r, k, blocks)
            acc[s] += plain_dot(ycat, high) + plain_dot(ycat, low)
    for b in range(blocks):
        out_e[b] = whole_of(acc[b])
        out_m[b] = whole_of(acc[blocks + b])
        out_o[b] = whole_of(acc[2 * blocks + b])


def forward(th, low, cols, y, y_o, y_e, x, dg, mk, *rest, reverses):
    reverse, (result, *kept, xcat) = rest[:reverses], rest[reverses:]
    blocks, slots = th.shape[0], th.shape[1]
    for b in range(blocks):
        xcat[b] = parts_of(y_e[b])
        xcat[blocks + b] = parts_of(y[b])
        xcat[2 * blocks + b] = parts_of(y_o[b])
    for r in range(blocks):
        total = jnp.zeros(xcat.shape[1:], f32)
        for k in range(slots):
            field = xcat[slot_of(cols, r, k, blocks)]
            matrix = low[r, k]
            if kept:
                matrix = matrix.T
                kept[0][r, k] = matrix
            total += plain_dot(field, th[r, k]) + plain_dot(field, matrix)
        summed = whole_of(total)
        for part in reverse:
            summed += part[r]
        result[r] = dg[r] * x[r] + mk[r] * summed


def reverse_second(kh, kl, cols, y1, r0, w, dg, mk, out_e, out_m, out_o, grams, acc):
    blocks, slots = kh.shape[0], kh.shape[1]
    n = y1.shape[1]
    acc[...] = jnp.zeros_like(acc)
    for r in range(blocks):
        ycat = parts_of(y1[r])
        for k in range(slots):
            s = slot_of(cols, r, k, blocks)
            acc[s] += plain_dot(ycat, kh[r, k]) + plain_dot(ycat, kl[r, k])
    total = jnp.zeros((3 * n, 4 * n), f32)
    for b in range(blocks):
        own = whole_of(acc[blocks + b])
        out_e[b] = whole_of(acc[b])
        out_m[b] = own
        out_o[b] = whole_of(acc[2 * blocks + b])
        free = mk[b] * own
        total += gram(
            jnp.concatenate([r0[b], w[b], free], axis=0),
            jnp.concatenate([r0[b], w[b], dg[b] * w[b], free], axis=0),
        )
    h12 = total[n : 2 * n, 2 * n : 3 * n] + total[n : 2 * n, 3 * n :] + total[2 * n :, n : 2 * n]
    rest = jnp.zeros((n, grams.shape[1] - 4 * n), f32)
    grams[...] = jnp.concatenate(
        [total[:n, : 2 * n], total[n : 2 * n, n : 2 * n], h12, rest], axis=1
    )


def halo_grams(out_e, out_o, y_o, y_e, grams, result):
    n = out_e.shape[1]
    total = jnp.zeros((2 * n, 2 * n), f32)
    for b in range(out_e.shape[0]):
        for out, y in ((out_e, y_e), (out_o, y_o)):
            total += gram(
                jnp.concatenate([out[b], y[b]], axis=0), jnp.concatenate([y[b], out[b]], axis=0)
            )
    cross = total[:n, :n] + total[n:, n:]
    before = jnp.zeros((n, 3 * n), f32)
    after = jnp.zeros((n, result.shape[1] - 4 * n), f32)
    result[...] = grams[...] + jnp.concatenate([before, cross, after], axis=1)


def eliminate(systems):
    count = systems[0][0].shape[0]
    rows = lax.broadcasted_iota(jnp.int32, (count, 128), 0)
    spread = [
        [jnp.broadcast_to(matrix[:, k : k + 1], (count, 128)) for k in range(count)]
        for matrix, _ in systems
    ]
    sides = [side for _, side in systems]
    for k in range(count):
        for i, columns in enumerate(spread):
            column = columns[k]
            scale = 1.0 / column[k : k + 1]

            def step(x):
                width = x.shape[1]
                pivot = x[k : k + 1] * scale[:, :width]
                return jnp.where(rows[:, :width] == k, pivot, x - column[:, :width] * pivot)

            spread[i] = [step(c) if j > k else c for j, c in enumerate(columns)]
            sides[i] = step(sides[i])
    return sides


def columns_of(matrix):
    return [matrix[:, k : k + 1] for k in range(matrix.shape[1])]


def small_dot(columns, right):
    terms = [column * right[k : k + 1, :] for k, column in enumerate(columns)]
    while len(terms) > 1:
        terms = [a + b for a, b in zip(terms[::2], terms[1::2])]
    return terms[0]


def finish(*refs, rounds, shift):
    gram_refs = refs[:rounds]
    r0, w, u, disp, resid = refs[rounds:]
    blocks, n = r0.shape[0], r0.shape[1]
    comps = disp.shape[0]
    bn = disp.shape[2] // blocks
    sums = gram_refs[0][...]
    for ref in gram_refs[1:]:
        sums += ref[...]
    h00, h01, h11, h12 = (sums[:, i * n : (i + 1) * n] for i in range(4))
    eye = (
        lax.broadcasted_iota(jnp.int32, (n, n), 0) == lax.broadcasted_iota(jnp.int32, (n, n), 1)
    ).astype(f32)
    first, inverse0 = eliminate(
        [(shift * h00 + h01, jnp.concatenate([h00, h01, eye], axis=1)), (h00, eye)]
    )
    step, keep, inverse = (first[:, i * n : (i + 1) * n] for i in range(3))
    c00, c01, c11, c12 = (columns_of(h) for h in (h00, h01, h11, h12))
    step_t, keep_t = small_dot(c00, inverse), small_dot(c01, inverse)
    h11s = small_dot(c11, step)
    past = h11s - small_dot(c01, keep)
    image = small_dot(c12, step) + shift * past - small_dot(c11, keep)
    both = small_dot(
        columns_of(step_t), jnp.concatenate([past, image, h11 + shift * h01], axis=1)
    )
    rho = both[:, :n]
    mixing = small_dot(columns_of(inverse0), rho)
    curvature = both[:, n : 2 * n] - small_dot(columns_of(both[:, 2 * n :]), mixing)
    rho_columns = columns_of(rho)
    lead_t = keep_t + small_dot(rho_columns, inverse0)
    after_t = small_dot(rho_columns, eliminate([(curvature, eye)])[0])
    moved = small_dot(columns_of(after_t), jnp.concatenate([lead_t, step_t], axis=1))
    lead_after, step_after = moved[:, :n], moved[:, n:]
    for_disp = (step_t + lead_after, -step_after)
    for_resid = (
        keep_t - shift * lead_after, shift * step_after - step_t - lead_after, step_after
    )
    for mix, out in ((for_disp, disp), (for_resid, resid)):
        mix_columns = [columns_of(m) for m in mix]
        for b in range(blocks):
            total = None
            for columns, x in zip(mix_columns, (r0, w, u)):
                for g in range(n):
                    term = columns[g] * x[b, g : g + 1, :]
                    total = term if total is None else total + term
            for c in range(comps):
                out[c, :, b * bn : (b + 1) * bn] = total[:, c * bn : (c + 1) * bn]


def even_swap(x):
    count = lax.axis_size("row")
    return lax.ppermute(x, "row", [(i, i ^ 1) for i in range(count)])


def odd_swap(x):
    groups, count = lax.axis_size("groups"), lax.axis_size("row")
    route = []
    for g in range(groups):
        for i in range(count):
            if i == 0 or i == count - 1:
                other = g ^ 1 if (g ^ 1) < groups else g
                route.append((g * count + i, other * count + i))
            else:
                route.append((g * count + i, g * count + ((i + 1) ^ 1) - 1))
    return lax.ppermute(x, ("groups", "row"), route)


def swapped_sums(x):
    count = lax.axis_size("row")
    base = 1
    while True:
        order = (1,3,2) if base == 1 else (1,3,2)
        masks = [m * base for m in order] if 2 * base < count else [base]
        got = [
            lax.ppermute(x, "row", [(i, i ^ mask) for i in range(count)]) for mask in masks
        ]
        base *= len(masks) + 1
        if base >= count:
            return [x, *got]
        x = x + sum(got)


def shards(coupling, columns, stiff_diag, interior, loads):
    blocks, slots, width = coupling.shape[0], coupling.shape[1], coupling.shape[2]
    fields, comps, nodes = loads.shape
    shift = slot_shift * slots + diag_middle
    flops = 8 * 2 * fields * blocks * slots * width * width
    field = jax.ShapeDtypeStruct((blocks, fields, width), f32)
    row = jax.ShapeDtypeStruct((blocks, 1, width), f32)
    half = jax.ShapeDtypeStruct(coupling.shape, bf16)
    gram_shape = jax.ShapeDtypeStruct((fields, 128), f32)
    acc = pltpu.VMEM((3 * blocks, 2 * fields, width), f32)
    cat = pltpu.VMEM((3 * blocks, 2 * fields, width), bf16)

    r0, y0, dg, mk = call(
        lambda *refs: prepare(*refs, blocks=blocks, shift=diag_middle),
        (field, field, row, row), [pl.BlockSpec(memory_space=pl.ANY)] * 3,
        [
            pltpu.VMEM((comps, fields, nodes), f32),
            pltpu.VMEM((nodes,), jnp.int32),
            pltpu.VMEM((comps, nodes), f32),
            pltpu.SemaphoreType.DMA((3,)),
        ],
        flops=10**10,
        name="prepare",
    )(*(in_hbm(x) for x in (loads.transpose(1, 0, 2), interior, stiff_diag)))
    y0_e, y0_o = even_swap(y0), odd_swap(y0)
    kh, kl, th, a_e, a_m, a_o = call(
        reverse_first, (half, half, half, field, field, field), [vmem, smem, vmem],
        [acc], flops, name="reverse_first",
    )(coupling, columns, y0)
    b_e, b_o = even_swap(a_e), odd_swap(a_o)
    wp, tl = call(
        functools.partial(forward, reverses=1), (field, half), [vmem, vmem, smem] + [vmem] * 7,
        [cat], flops, name="forward_first",
    )(th, kl, columns, y0, y0_o, y0_e, r0, dg, mk, a_m)
    w = wp + mk * (b_o + b_e)
    y1 = w * mk
    y1_e, y1_o = even_swap(y1), odd_swap(y1)
    c_e, c_m, c_o, grams = call(
        reverse_second, (field, field, field, gram_shape), [vmem, vmem, smem] + [vmem] * 5,
        [acc], flops, name="reverse_second",
    )(kh, kl, columns, y1, r0, w, dg, mk)
    grams = call(halo_grams, gram_shape, [vmem] * 5, name="halo_grams")(
        c_e, c_o, y1_o, y1_e, grams
    )
    sums = swapped_sums(grams)
    d_e, d_o = even_swap(c_e), odd_swap(c_o)
    u = call(
        functools.partial(forward, reverses=3), field, [vmem, vmem, smem] + [vmem] * 9,
        [cat], flops, name="forward_second",
    )(th, tl, columns, y1, y1_o, y1_e, w, dg, mk, c_m, d_o, d_e)
    out = jax.ShapeDtypeStruct((comps, fields, nodes), f32)
    disp, resid = call(
        lambda *refs: finish(*refs, rounds=len(sums), shift=shift),
        (out, out), [vmem] * (len(sums) + 3), name="finish",
    )(*sums, r0, w, u)
    return disp.transpose(1, 0, 2), resid.transpose(1, 0, 2)


def solution(mesh):
    placed = (
        P(("groups", "row"), None, None, None),
        P(("groups", "row"), None),
        P(None, ("groups", "row")),
        P(("groups", "row")),
        P(None, None, ("groups", "row")),
    )
    return jax.shard_map(
        shards,
        mesh=mesh,
        in_specs=placed,
        out_specs=(P(None, None, ("groups", "row")), P(None, None, ("groups", "row"))),
        check_vma=False,
    )
```

```python
import functools

import jax
import jax.numpy as jnp
from jax import lax
from jax.experimental import pallas as pl
from jax.experimental.pallas import tpu as pltpu
from jax.sharding import PartitionSpec as P

f32 = jnp.float32
bf16 = jnp.bfloat16
slot_shift = 1.2
diag_middle = 1.25


def call(body, out_shape, in_specs, scratch=(), flops=0, name=None, limit=24):
    return pl.pallas_call(
        body,
        out_shape=out_shape,
        in_specs=in_specs,
        out_specs=jax.tree.map(lambda _: pl.BlockSpec(memory_space=pltpu.VMEM), out_shape),
        scratch_shapes=list(scratch),
        compiler_params=pltpu.CompilerParams(vmem_limit_bytes=limit * 2**20),
        cost_estimate=pl.CostEstimate(flops=flops, bytes_accessed=2**20, transcendentals=0),
        name=name,
    )


vmem = pl.BlockSpec(memory_space=pltpu.VMEM)
smem = pl.BlockSpec(memory_space=pltpu.SMEM)


def in_hbm(x):
    return pltpu.with_memory_space_constraint(x, pltpu.HBM)


def thirds_of(x):
    high = x.astype(bf16).astype(f32)
    rest = x - high
    middle = rest.astype(bf16).astype(f32)
    return jnp.concatenate([high, middle, rest - middle], axis=0).astype(bf16)


def gram(left, right):
    a, b = left.shape[0], right.shape[0]
    parts = turned_dot(thirds_of(left), thirds_of(right))
    rows = parts[:a] + (parts[a : 2 * a] + parts[2 * a :])
    return rows[:, :b] + (rows[:, b : 2 * b] + rows[:, 2 * b :])


def parts_of(x):
    high = x.astype(bf16).astype(f32)
    return jnp.concatenate([high, x - high], axis=0).astype(bf16)


def whole_of(x16):
    half = x16.shape[0] // 2
    return x16[:half] + x16[half:]


def plain_dot(x, matrix):
    return lax.dot_general(x, matrix, (((1,), (0,)), ((), ())), preferred_element_type=f32)


def turned_dot(x, matrix):
    return lax.dot_general(x, matrix, (((1,), (1,)), ((), ())), preferred_element_type=f32)


def slot_of(cols, r, k, blocks):
    me = lax.axis_index("row")
    place = cols[r, k] - (me - 1) * blocks
    low = place < blocks
    high = place >= 2 * blocks
    swapped = jnp.where(low, place + 2 * blocks, jnp.where(high, place - 2 * blocks, place))
    return jnp.where(me % 2 == 0, swapped, place)


def prepare(
    loads_in, interior_in, stiff_in, r0, y0, wide, dg, mk, loads, interior, stiff, sems, *, blocks, shift
):
    comps = loads.shape[0]
    bn = loads.shape[2] // blocks
    fetches = [
        pltpu.make_async_copy(source, target, sems.at[i])
        for i, (source, target) in enumerate(
            ((loads_in, loads), (interior_in, interior), (stiff_in, stiff))
        )
    ]
    for fetch in fetches:
        fetch.start()
    for fetch in fetches:
        fetch.wait()
    inside_all = interior[...].astype(f32).reshape(1, -1)
    for b in range(blocks):
        nodes = pl.ds(b * bn, bn)
        inside = inside_all[:, b * bn : (b + 1) * bn]
        inside = jnp.concatenate([inside] * comps, axis=1)
        field = jnp.concatenate([loads[c, :, nodes] for c in range(comps)], axis=1)
        own = jnp.concatenate([stiff[c : c + 1, nodes] for c in range(comps)], axis=1)
        r0[b] = field
        y0[b] = field * inside
        wide[b, :, : y0.shape[2]] = field * inside
        wide[b, :, y0.shape[2] :] = jnp.zeros((wide.shape[1], wide.shape[2] - y0.shape[2]), f32)
        mk[b] = inside
        dg[b] = own - shift


def split(matrix):
    high = matrix.astype(bf16)
    return high, (matrix - high.astype(f32)).astype(bf16)


def reverse_products(coupling, cols, y, acc, th=None):
    blocks, slots = coupling.shape[0], coupling.shape[1]
    acc[...] = jnp.zeros_like(acc)
    for r in range(blocks):
        ycat = parts_of(y[r])
        for k in range(slots):
            high, low = split(coupling[r, k])
            if th is not None:
                th[r, k] = high.T
            s = slot_of(cols, r, k, blocks)
            acc[s] += whole_of(plain_dot(ycat, high) + plain_dot(ycat, low))


def reverse_first(coupling, cols, y0, th, out_e, out_m, out_o, acc):
    blocks = y0.shape[0]
    reverse_products(coupling, cols, y0, acc, th)
    for b in range(blocks):
        out_e[b] = acc[b]
        out_m[b] = acc[blocks + b]
        out_o[b] = acc[2 * blocks + b]


def forward(th, source, cols, y, y_o, y_e, x, dg, mk, *rest, reverses):
    reverse, (result, *kept, xcat) = rest[:reverses], rest[reverses:]
    blocks, slots = th.shape[0], th.shape[1]
    for b in range(blocks):
        xcat[b] = parts_of(y_e[b])
        xcat[blocks + b] = parts_of(y[b])
        xcat[2 * blocks + b] = parts_of(y_o[b, :, : y.shape[2]])
    for r in range(blocks):
        total = jnp.zeros(xcat.shape[1:], f32)
        for k in range(slots):
            field = xcat[slot_of(cols, r, k, blocks)]
            low = source[r, k]
            if kept:
                low = split(low)[1].T
                kept[0][r, k] = low
            total += plain_dot(field, th[r, k]) + plain_dot(field, low)
        summed = whole_of(total)
        for part in reverse:
            summed += part[r, :, : y.shape[2]]
        result[r] = dg[r] * x[r] + mk[r] * summed


def reverse_second(coupling, cols, y1, r0, w, dg, out_e, out_m, out_o, grams, acc):
    blocks, n = y1.shape[0], y1.shape[1]
    total = jnp.zeros((2 * n, 3 * n), f32)
    for b in range(blocks):
        total += gram(
            jnp.concatenate([r0[b], w[b]], axis=0),
            jnp.concatenate([r0[b], w[b], dg[b] * w[b]], axis=0),
        )
    rest = jnp.zeros((n, grams.shape[1] - 4 * n), f32)
    grams[...] = jnp.concatenate([total[:n, : 2 * n], total[n:, n:], rest], axis=1)
    reverse_products(coupling, cols, y1, acc)
    for b in range(blocks):
        out_e[b] = acc[b]
        out_m[b] = acc[blocks + b]
        out_o[b] = acc[2 * blocks + b]


def cross_grams(out_e, out_m, out_o, y_e, y, y_o, grams, result):
    n, width = y.shape[1], y.shape[2]
    one = other = jnp.zeros((2 * n, 2 * n), f32)
    for b in range(y.shape[0]):
        for out, field in ((out_m, y), (out_e, y_e), (out_o, y_o)):
            sent, seen = parts_of(out[b]), parts_of(field[b, :, :width])
            one += turned_dot(sent, seen)
            other += turned_dot(seen, sent)
    both = whole_of(one + other)
    cross = both[:, :n] + both[:, n:]
    before = jnp.zeros((n, 3 * n), f32)
    after = jnp.zeros((n, result.shape[1] - 4 * n), f32)
    result[...] = grams[...] + jnp.concatenate([before, cross, after], axis=1)


def eliminate(systems):
    count = systems[0][0].shape[0]
    rows = lax.broadcasted_iota(jnp.int32, (count, 128), 0)
    spread = [
        [jnp.broadcast_to(matrix[:, k : k + 1], (count, 128)) for k in range(count)]
        for matrix, _ in systems
    ]
    sides = [side for _, side in systems]
    for k in range(count):
        for i, columns in enumerate(spread):
            column = columns[k]
            scale = 1.0 / column[k : k + 1]

            def step(x):
                width = x.shape[1]
                pivot = x[k : k + 1] * scale[:, :width]
                return jnp.where(rows[:, :width] == k, pivot, x - column[:, :width] * pivot)

            spread[i] = [step(c) if j > k else c for j, c in enumerate(columns)]
            sides[i] = step(sides[i])
    return sides


def columns_of(matrix):
    return [matrix[:, k : k + 1] for k in range(matrix.shape[1])]


def small_dot(columns, right):
    terms = [column * right[k : k + 1, :] for k, column in enumerate(columns)]
    while len(terms) > 1:
        terms = [a + b for a, b in zip(terms[::2], terms[1::2])]
    return terms[0]


def finish(*refs, rounds, shift):
    gram_refs = refs[:rounds]
    r0, w, u, disp, resid = refs[rounds:]
    blocks, n = r0.shape[0], r0.shape[1]
    comps = disp.shape[0]
    bn = disp.shape[2] // blocks
    sums = gram_refs[0][...]
    for ref in gram_refs[1:]:
        sums += ref[:, : sums.shape[1]]
    h00, h01, h11, h12 = (sums[:, i * n : (i + 1) * n] for i in range(4))
    eye = (
        lax.broadcasted_iota(jnp.int32, (n, n), 0) == lax.broadcasted_iota(jnp.int32, (n, n), 1)
    ).astype(f32)
    first, inverse0 = eliminate(
        [(shift * h00 + h01, jnp.concatenate([h00, h01, eye], axis=1)), (h00, eye)]
    )
    step, keep, inverse = (first[:, i * n : (i + 1) * n] for i in range(3))
    c00, c01, c11, c12 = (columns_of(h) for h in (h00, h01, h11, h12))
    step_t, keep_t = small_dot(c00, inverse), small_dot(c01, inverse)
    h11s = small_dot(c11, step)
    past = h11s - small_dot(c01, keep)
    image = small_dot(c12, step) + shift * past - small_dot(c11, keep)
    both = small_dot(
        columns_of(step_t), jnp.concatenate([past, image, h11 + shift * h01], axis=1)
    )
    rho = both[:, :n]
    mixing = small_dot(columns_of(inverse0), rho)
    curvature = both[:, n : 2 * n] - small_dot(columns_of(both[:, 2 * n :]), mixing)
    rho_columns = columns_of(rho)
    lead_t = keep_t + small_dot(rho_columns, inverse0)
    after_t = small_dot(rho_columns, eliminate([(curvature, eye)])[0])
    moved = small_dot(columns_of(after_t), jnp.concatenate([lead_t, step_t], axis=1))
    lead_after, step_after = moved[:, :n], moved[:, n:]
    for_disp = (step_t + lead_after, -step_after)
    for_resid = (
        keep_t - shift * lead_after, shift * step_after - step_t - lead_after, step_after
    )
    for mix, out in ((for_disp, disp), (for_resid, resid)):
        mix_columns = [columns_of(m) for m in mix]
        for b in range(blocks):
            total = None
            for columns, x in zip(mix_columns, (r0, w, u)):
                for g in range(n):
                    term = columns[g] * x[b, g : g + 1, :]
                    total = term if total is None else total + term
            for c in range(comps):
                out[c, :, b * bn : (b + 1) * bn] = total[:, c * bn : (c + 1) * bn]


def widened(x):
    return jnp.pad(x, ((0, 0), (0, 0), (0, 64)))


def even_swap(x):
    count = lax.axis_size("row")
    return lax.ppermute(x, "row", [(i, i ^ 1) for i in range(count)])


def odd_swap(x):
    groups, count = lax.axis_size("groups"), lax.axis_size("row")
    route = []
    for g in range(groups):
        for i in range(count):
            if i == 0 or i == count - 1:
                other = g ^ 1 if (g ^ 1) < groups else g
                route.append((g * count + i, other * count + i))
            else:
                route.append((g * count + i, g * count + ((i + 1) ^ 1) - 1))
    return lax.ppermute(x, ("groups", "row"), route)


def swapped_sums(x):
    count = lax.axis_size("row")
    width = x.shape[1]
    base = 1
    while True:
        masks = [base, 2 * base, 3 * base] if 2 * base < count else [base]
        got = []
        for i, mask in enumerate(masks):
            sent = jnp.pad(x, ((0, 0), (0, (len(masks) - 1 - i) * width))) if base > 1 else x
            route = [(j, j ^ mask) for j in range(count)]
            got.append(lax.ppermute(sent, "row", route))
        base *= len(masks) + 1
        if base >= count:
            return [x, *got]
        x = x + sum(g[:, :width] for g in got)


def shards(coupling, columns, stiff_diag, interior, loads):
    blocks, slots, width = coupling.shape[0], coupling.shape[1], coupling.shape[2]
    fields, comps, nodes = loads.shape
    shift = slot_shift * slots + diag_middle
    flops = 8 * 2 * fields * blocks * slots * width * width
    field = jax.ShapeDtypeStruct((blocks, fields, width), f32)
    wide = jax.ShapeDtypeStruct((blocks, fields, width + 64), f32)
    row = jax.ShapeDtypeStruct((blocks, 1, width), f32)
    half = jax.ShapeDtypeStruct(coupling.shape, bf16)
    gram_shape = jax.ShapeDtypeStruct((fields, 128), f32)
    acc = pltpu.VMEM((3 * blocks, fields, width), f32)
    cat = pltpu.VMEM((3 * blocks, 2 * fields, width), bf16)

    r0, y0, wide0, dg, mk = call(
        lambda *refs: prepare(*refs, blocks=blocks, shift=diag_middle),
        (field, field, wide, row, row), [pl.BlockSpec(memory_space=pl.ANY)] * 3,
        [
            pltpu.VMEM((comps, fields, nodes), f32),
            pltpu.VMEM((nodes,), jnp.int32),
            pltpu.VMEM((comps, nodes), f32),
            pltpu.SemaphoreType.DMA((3,)),
        ],
        flops=10**10,
        name="prepare",
    )(*(in_hbm(x) for x in (loads.transpose(1, 0, 2), interior, stiff_diag)))
    y0_e, y0_o = even_swap(y0), odd_swap(wide0)
    th, a_e, a_m, a_o = call(
        reverse_first, (half, field, field, field), [vmem, smem, vmem],
        [acc], flops, name="reverse_first",
    )(coupling, columns, y0)
    b_e, b_o = even_swap(a_e), odd_swap(a_o)
    wp, tl = call(
        functools.partial(forward, reverses=1), (field, half), [vmem, vmem, smem] + [vmem] * 7,
        [cat], flops, name="forward_first",
    )(th, coupling, columns, y0, y0_o, y0_e, r0, dg, mk, a_m)
    w = wp + mk * (b_o + b_e)
    y1 = w * mk
    y1_e, y1_o = even_swap(y1), odd_swap(widened(y1))
    c_e, c_m, c_o, grams = call(
        reverse_second, (field, field, field, gram_shape), [vmem, smem] + [vmem] * 4,
        [acc], flops, name="reverse_second",
    )(coupling, columns, y1, r0, w, dg)
    grams = call(cross_grams, gram_shape, [vmem] * 7, name="cross_grams")(
        c_e, c_m, c_o, y1_e, y1, y1_o, grams
    )
    sums = swapped_sums(grams)
    d_e, d_o = even_swap(c_e), odd_swap(c_o)
    u = call(
        functools.partial(forward, reverses=3), field, [vmem, vmem, smem] + [vmem] * 9,
        [cat], flops, name="forward_second",
    )(th, tl, columns, y1, y1_o, y1_e, w, dg, mk, c_m, d_o, d_e)
    out = jax.ShapeDtypeStruct((comps, fields, nodes), f32)
    disp, resid = call(
        lambda *refs: finish(*refs, rounds=len(sums), shift=shift),
        (out, out), [vmem] * (len(sums) + 3), name="finish",
    )(*sums, r0, w, u)
    return disp.transpose(1, 0, 2), resid.transpose(1, 0, 2)


def solution(mesh):
    placed = (
        P(("groups", "row"), None, None, None),
        P(("groups", "row"), None),
        P(None, ("groups", "row")),
        P(("groups", "row")),
        P(None, None, ("groups", "row")),
    )
    return jax.shard_map(
        shards,
        mesh=mesh,
        in_specs=placed,
        out_specs=(P(None, None, ("groups", "row")), P(None, None, ("groups", "row"))),
        check_vma=False,
    )
```

```python
import functools

import jax
import jax.numpy as jnp
from jax import lax
from jax.experimental import pallas as pl
from jax.experimental.pallas import tpu as pltpu
from jax.sharding import PartitionSpec as P

f32 = jnp.float32
bf16 = jnp.bfloat16
slot_shift = 1.2
diag_middle = 1.25


def call(body, out_shape, in_specs, scratch=(), flops=0, name=None, limit=24):
    return pl.pallas_call(
        body,
        out_shape=out_shape,
        in_specs=in_specs,
        out_specs=jax.tree.map(lambda _: pl.BlockSpec(memory_space=pltpu.VMEM), out_shape),
        scratch_shapes=list(scratch),
        compiler_params=pltpu.CompilerParams(vmem_limit_bytes=limit * 2**20),
        cost_estimate=pl.CostEstimate(flops=flops, bytes_accessed=2**20, transcendentals=0),
        name=name,
    )


vmem = pl.BlockSpec(memory_space=pltpu.VMEM)
smem = pl.BlockSpec(memory_space=pltpu.SMEM)


def in_hbm(x):
    return pltpu.with_memory_space_constraint(x, pltpu.HBM)


def thirds_of(x):
    high = x.astype(bf16).astype(f32)
    rest = x - high
    middle = rest.astype(bf16).astype(f32)
    return jnp.concatenate([high, middle, rest - middle], axis=0).astype(bf16)


def gram(left, right):
    a, b = left.shape[0], right.shape[0]
    parts = turned_dot(thirds_of(left), thirds_of(right))
    rows = parts[:a] + (parts[a : 2 * a] + parts[2 * a :])
    return rows[:, :b] + (rows[:, b : 2 * b] + rows[:, 2 * b :])


def parts_of(x):
    high = x.astype(bf16).astype(f32)
    return jnp.concatenate([high, x - high], axis=0).astype(bf16)


def whole_of(x16):
    half = x16.shape[0] // 2
    return x16[:half] + x16[half:]


def plain_dot(x, matrix):
    return lax.dot_general(x, matrix, (((1,), (0,)), ((), ())), preferred_element_type=f32)


def turned_dot(x, matrix):
    return lax.dot_general(x, matrix, (((1,), (1,)), ((), ())), preferred_element_type=f32)


def slot_of(cols, r, k, blocks):
    me = lax.axis_index("row")
    place = cols[r, k] - (me - 1) * blocks
    low = place < blocks
    high = place >= 2 * blocks
    swapped = jnp.where(low, place + 2 * blocks, jnp.where(high, place - 2 * blocks, place))
    return jnp.where(me % 2 == 0, swapped, place)


def prepare(
    loads_in, interior_in, stiff_in, r0, y0, wide, dg, mk, loads, interior, stiff, sems, *, blocks, shift
):
    comps = loads.shape[0]
    bn = loads.shape[2] // blocks
    fetches = [
        pltpu.make_async_copy(source, target, sems.at[i])
        for i, (source, target) in enumerate(
            ((loads_in, loads), (interior_in, interior), (stiff_in, stiff))
        )
    ]
    for fetch in fetches:
        fetch.start()
    for fetch in fetches:
        fetch.wait()
    inside_all = interior[...].astype(f32).reshape(1, -1)
    for b in range(blocks):
        nodes = pl.ds(b * bn, bn)
        inside = inside_all[:, b * bn : (b + 1) * bn]
        inside = jnp.concatenate([inside] * comps, axis=1)
        field = jnp.concatenate([loads[c, :, nodes] for c in range(comps)], axis=1)
        own = jnp.concatenate([stiff[c : c + 1, nodes] for c in range(comps)], axis=1)
        r0[b] = field
        y0[b] = field * inside
        wide[b, :, : y0.shape[2]] = field * inside
        wide[b, :, y0.shape[2] :] = jnp.zeros((wide.shape[1], wide.shape[2] - y0.shape[2]), f32)
        mk[b] = inside
        dg[b] = own - shift


def split(matrix):
    high = matrix.astype(bf16)
    return high, (matrix - high.astype(f32)).astype(bf16)


def reverse_products(coupling, cols, y, acc, th=None):
    blocks, slots = coupling.shape[0], coupling.shape[1]
    acc[...] = jnp.zeros_like(acc)
    for r in range(blocks):
        ycat = parts_of(y[r])
        for k in range(slots):
            high, low = split(coupling[r, k])
            if th is not None:
                th[r, k] = high.T
            s = slot_of(cols, r, k, blocks)
            acc[s] += whole_of(plain_dot(ycat, high) + plain_dot(ycat, low))


def reverse_first(coupling, cols, y0, th, out_e, out_m, out_o, acc):
    blocks = y0.shape[0]
    reverse_products(coupling, cols, y0, acc, th)
    for b in range(blocks):
        out_e[b] = acc[b]
        out_m[b] = acc[blocks + b]
        out_o[b] = acc[2 * blocks + b]


def forward(th, source, cols, y, y_o, y_e, x, dg, mk, *rest, reverses):
    reverse, (result, *kept, xcat) = rest[:reverses], rest[reverses:]
    blocks, slots = th.shape[0], th.shape[1]
    for b in range(blocks):
        xcat[b] = parts_of(y_e[b])
        xcat[blocks + b] = parts_of(y[b])
        xcat[2 * blocks + b] = parts_of(y_o[b, :, : y.shape[2]])
    for r in range(blocks):
        total = jnp.zeros(xcat.shape[1:], f32)
        for k in range(slots):
            field = xcat[slot_of(cols, r, k, blocks)]
            low = source[r, k]
            if kept:
                low = split(low)[1].T
                kept[0][r, k] = low
            total += plain_dot(field, th[r, k]) + plain_dot(field, low)
        summed = whole_of(total)
        for part in reverse:
            summed += part[r, :, : y.shape[2]]
        result[r] = dg[r] * x[r] + mk[r] * summed


def reverse_second(coupling, cols, y1, r0, w, dg, out_e, out_m, out_o, grams, acc):
    blocks, n = y1.shape[0], y1.shape[1]
    total = jnp.zeros((2 * n, 3 * n), f32)
    for b in range(blocks):
        total += gram(
            jnp.concatenate([r0[b], w[b]], axis=0),
            jnp.concatenate([r0[b], w[b], dg[b] * w[b]], axis=0),
        )
    rest = jnp.zeros((n, grams.shape[1] - 4 * n), f32)
    grams[...] = jnp.concatenate([total[:n, : 2 * n], total[n:, n:], rest], axis=1)
    reverse_products(coupling, cols, y1, acc)
    for b in range(blocks):
        out_e[b] = acc[b]
        out_m[b] = acc[blocks + b]
        out_o[b] = acc[2 * blocks + b]


def cross_grams(out_e, out_m, out_o, y_e, y, y_o, grams, result):
    n, width = y.shape[1], y.shape[2]
    one = other = jnp.zeros((2 * n, 2 * n), f32)
    for b in range(y.shape[0]):
        for out, field in ((out_m, y), (out_e, y_e), (out_o, y_o)):
            sent, seen = parts_of(out[b]), parts_of(field[b, :, :width])
            one += turned_dot(sent, seen)
            other += turned_dot(seen, sent)
    both = whole_of(one + other)
    cross = both[:, :n] + both[:, n:]
    before = jnp.zeros((n, 3 * n), f32)
    after = jnp.zeros((n, result.shape[1] - 4 * n), f32)
    result[...] = grams[...] + jnp.concatenate([before, cross, after], axis=1)


def eliminate(systems):
    count = systems[0][0].shape[0]
    rows = lax.broadcasted_iota(jnp.int32, (count, 128), 0)
    spread = [
        [jnp.broadcast_to(matrix[:, k : k + 1], (count, 128)) for k in range(count)]
        for matrix, _ in systems
    ]
    sides = [side for _, side in systems]
    for k in range(count):
        for i, columns in enumerate(spread):
            column = columns[k]
            scale = 1.0 / column[k : k + 1]

            def step(x):
                width = x.shape[1]
                pivot = x[k : k + 1] * scale[:, :width]
                return jnp.where(rows[:, :width] == k, pivot, x - column[:, :width] * pivot)

            spread[i] = [step(c) if j > k else c for j, c in enumerate(columns)]
            sides[i] = step(sides[i])
    return sides


def columns_of(matrix):
    return [matrix[:, k : k + 1] for k in range(matrix.shape[1])]


def small_dot(columns, right):
    terms = [column * right[k : k + 1, :] for k, column in enumerate(columns)]
    while len(terms) > 1:
        terms = [a + b for a, b in zip(terms[::2], terms[1::2])]
    return terms[0]


def finish(*refs, rounds, shift):
    gram_refs = refs[:rounds]
    r0, w, u, disp, resid = refs[rounds:]
    blocks, n = r0.shape[0], r0.shape[1]
    comps = disp.shape[0]
    bn = disp.shape[2] // blocks
    sums = gram_refs[0][...]
    for ref in gram_refs[1:]:
        sums += ref[:, : sums.shape[1]]
    h00, h01, h11, h12 = (sums[:, i * n : (i + 1) * n] for i in range(4))
    eye = (
        lax.broadcasted_iota(jnp.int32, (n, n), 0) == lax.broadcasted_iota(jnp.int32, (n, n), 1)
    ).astype(f32)
    first, inverse0 = eliminate(
        [(shift * h00 + h01, jnp.concatenate([h00, h01, eye], axis=1)), (h00, eye)]
    )
    step, keep, inverse = (first[:, i * n : (i + 1) * n] for i in range(3))
    c00, c01, c11, c12 = (columns_of(h) for h in (h00, h01, h11, h12))
    step_t, keep_t = small_dot(c00, inverse), small_dot(c01, inverse)
    h11s = small_dot(c11, step)
    past = h11s - small_dot(c01, keep)
    image = small_dot(c12, step) + shift * past - small_dot(c11, keep)
    onward = small_dot(columns_of(h11 + shift * h01), inverse0)
    both = small_dot(columns_of(step_t), jnp.concatenate([past, image, onward], axis=1))
    rho = both[:, :n]
    curvature = both[:, n : 2 * n] - small_dot(columns_of(both[:, 2 * n :]), rho)
    rho_columns = columns_of(rho)
    lead_t = keep_t + small_dot(rho_columns, inverse0)
    solved = eliminate([(curvature, jnp.concatenate([lead_t, step_t], axis=1))])[0]
    moved = small_dot(rho_columns, solved)
    lead_after, step_after = moved[:, :n], moved[:, n:]
    for_disp = (step_t + lead_after, -step_after)
    for_resid = (
        keep_t - shift * lead_after, shift * step_after - step_t - lead_after, step_after
    )
    for mix, out in ((for_disp, disp), (for_resid, resid)):
        mix_columns = [columns_of(m) for m in mix]
        for b in range(blocks):
            total = None
            for columns, x in zip(mix_columns, (r0, w, u)):
                for g in range(n):
                    term = columns[g] * x[b, g : g + 1, :]
                    total = term if total is None else total + term
            for c in range(comps):
                out[c, :, b * bn : (b + 1) * bn] = total[:, c * bn : (c + 1) * bn]


def widened(x):
    return jnp.pad(x, ((0, 0), (0, 0), (0, 64)))


def even_swap(x):
    count = lax.axis_size("row")
    return lax.ppermute(x, "row", [(i, i ^ 1) for i in range(count)])


def odd_swap(x):
    groups, count = lax.axis_size("groups"), lax.axis_size("row")
    route = []
    for g in range(groups):
        for i in range(count):
            if i == 0 or i == count - 1:
                other = g ^ 1 if (g ^ 1) < groups else g
                route.append((g * count + i, other * count + i))
            else:
                route.append((g * count + i, g * count + ((i + 1) ^ 1) - 1))
    return lax.ppermute(x, ("groups", "row"), route)


def swapped_sums(x):
    count = lax.axis_size("row")
    width = x.shape[1]
    base = 1
    while True:
        cross = 1 if base > 1 else 0
        masks = [base, 2 * base + cross, 3 * base + cross] if 2 * base < count else [base]
        got = []
        for i, mask in enumerate(masks):
            extra = (len(masks) - 1 - i) * width if base > 1 else 0
            sent = jnp.pad(x, ((0, 0), (0, extra))) if extra else x
            route = [(j, j ^ mask) for j in range(count)]
            got.append(lax.ppermute(sent, "row", route))
        base *= len(masks) + 1
        if base >= count:
            return [x, *got]
        x = x + sum(g[:, :width] for g in got)


def shards(coupling, columns, stiff_diag, interior, loads):
    blocks, slots, width = coupling.shape[0], coupling.shape[1], coupling.shape[2]
    fields, comps, nodes = loads.shape
    shift = slot_shift * slots + diag_middle
    flops = 8 * 2 * fields * blocks * slots * width * width
    field = jax.ShapeDtypeStruct((blocks, fields, width), f32)
    wide = jax.ShapeDtypeStruct((blocks, fields, width + 64), f32)
    row = jax.ShapeDtypeStruct((blocks, 1, width), f32)
    half = jax.ShapeDtypeStruct(coupling.shape, bf16)
    gram_shape = jax.ShapeDtypeStruct((fields, 128), f32)
    acc = pltpu.VMEM((3 * blocks, fields, width), f32)
    cat = pltpu.VMEM((3 * blocks, 2 * fields, width), bf16)

    r0, y0, wide0, dg, mk = call(
        lambda *refs: prepare(*refs, blocks=blocks, shift=diag_middle),
        (field, field, wide, row, row), [pl.BlockSpec(memory_space=pl.ANY)] * 3,
        [
            pltpu.VMEM((comps, fields, nodes), f32),
            pltpu.VMEM((nodes,), jnp.int32),
            pltpu.VMEM((comps, nodes), f32),
            pltpu.SemaphoreType.DMA((3,)),
        ],
        flops=10**10,
        name="prepare",
    )(*(in_hbm(x) for x in (loads.transpose(1, 0, 2), interior, stiff_diag)))
    y0_e, y0_o = even_swap(y0), odd_swap(wide0)
    th, a_e, a_m, a_o = call(
        reverse_first, (half, field, field, field), [vmem, smem, vmem],
        [acc], flops, name="reverse_first",
    )(coupling, columns, y0)
    b_e, b_o = even_swap(a_e), odd_swap(a_o)
    wp, tl = call(
        functools.partial(forward, reverses=1), (field, half), [vmem, vmem, smem] + [vmem] * 7,
        [cat], flops, name="forward_first",
    )(th, coupling, columns, y0, y0_o, y0_e, r0, dg, mk, a_m)
    w = wp + mk * (b_o + b_e)
    y1 = w * mk
    y1_e, y1_o = even_swap(y1), odd_swap(widened(y1))
    c_e, c_m, c_o, grams = call(
        reverse_second, (field, field, field, gram_shape), [vmem, smem] + [vmem] * 4,
        [acc], flops, name="reverse_second",
    )(coupling, columns, y1, r0, w, dg)
    grams = call(cross_grams, gram_shape, [vmem] * 7, name="cross_grams")(
        c_e, c_m, c_o, y1_e, y1, y1_o, grams
    )
    sums = swapped_sums(grams)
    d_e, d_o = even_swap(c_e), odd_swap(c_o)
    u = call(
        functools.partial(forward, reverses=3), field, [vmem, vmem, smem] + [vmem] * 9,
        [cat], flops, name="forward_second",
    )(th, tl, columns, y1, y1_o, y1_e, w, dg, mk, c_m, d_o, d_e)
    out = jax.ShapeDtypeStruct((comps, fields, nodes), f32)
    disp, resid = call(
        lambda *refs: finish(*refs, rounds=len(sums), shift=shift),
        (out, out), [vmem] * (len(sums) + 3), name="finish",
    )(*sums, r0, w, u)
    return disp.transpose(1, 0, 2), resid.transpose(1, 0, 2)


def solution(mesh):
    placed = (
        P(("groups", "row"), None, None, None),
        P(("groups", "row"), None),
        P(None, ("groups", "row")),
        P(("groups", "row")),
        P(None, None, ("groups", "row")),
    )
    return jax.shard_map(
        shards,
        mesh=mesh,
        in_specs=placed,
        out_specs=(P(None, None, ("groups", "row")), P(None, None, ("groups", "row"))),
        check_vma=False,
    )
```

```python
import functools

import jax
import jax.numpy as jnp
from jax import lax
from jax.experimental import pallas as pl
from jax.experimental.pallas import tpu as pltpu
from jax.sharding import PartitionSpec as P

f32 = jnp.float32
bf16 = jnp.bfloat16
slot_shift = 1.2
diag_middle = 1.25


def call(body, out_shape, in_specs, scratch=(), flops=0, name=None, limit=24):
    return pl.pallas_call(
        body,
        out_shape=out_shape,
        in_specs=in_specs,
        out_specs=jax.tree.map(lambda _: pl.BlockSpec(memory_space=pltpu.VMEM), out_shape),
        scratch_shapes=list(scratch),
        compiler_params=pltpu.CompilerParams(vmem_limit_bytes=limit * 2**20),
        cost_estimate=pl.CostEstimate(flops=flops, bytes_accessed=2**20, transcendentals=0),
        name=name,
    )


vmem = pl.BlockSpec(memory_space=pltpu.VMEM)
smem = pl.BlockSpec(memory_space=pltpu.SMEM)


def in_hbm(x):
    return pltpu.with_memory_space_constraint(x, pltpu.HBM)


def thirds_of(x):
    high = x.astype(bf16).astype(f32)
    rest = x - high
    middle = rest.astype(bf16).astype(f32)
    return jnp.concatenate([high, middle, rest - middle], axis=0).astype(bf16)


def gram(left, right):
    a, b = left.shape[0], right.shape[0]
    parts = turned_dot(thirds_of(left), thirds_of(right))
    rows = parts[:a] + (parts[a : 2 * a] + parts[2 * a :])
    return rows[:, :b] + (rows[:, b : 2 * b] + rows[:, 2 * b :])


def parts_of(x):
    high = x.astype(bf16).astype(f32)
    return jnp.concatenate([high, x - high], axis=0).astype(bf16)


def whole_of(x16):
    half = x16.shape[0] // 2
    return x16[:half] + x16[half:]


def plain_dot(x, matrix):
    return lax.dot_general(x, matrix, (((1,), (0,)), ((), ())), preferred_element_type=f32)


def turned_dot(x, matrix):
    return lax.dot_general(x, matrix, (((1,), (1,)), ((), ())), preferred_element_type=f32)


def slot_of(cols, r, k, blocks):
    me = lax.axis_index("row")
    place = cols[r, k] - (me - 1) * blocks
    low = place < blocks
    high = place >= 2 * blocks
    swapped = jnp.where(low, place + 2 * blocks, jnp.where(high, place - 2 * blocks, place))
    return jnp.where(me % 2 == 0, swapped, place)


def prepare(
    loads_in, interior_in, stiff_in, r0, y0, wide, dg, mk, loads, interior, stiff, sems, *, blocks, shift
):
    comps = loads.shape[0]
    bn = loads.shape[2] // blocks
    fetches = [
        pltpu.make_async_copy(source, target, sems.at[i])
        for i, (source, target) in enumerate(
            ((loads_in, loads), (interior_in, interior), (stiff_in, stiff))
        )
    ]
    for fetch in fetches:
        fetch.start()
    for fetch in fetches:
        fetch.wait()
    inside_all = interior[...].astype(f32).reshape(1, -1)
    for b in range(blocks):
        nodes = pl.ds(b * bn, bn)
        inside = inside_all[:, b * bn : (b + 1) * bn]
        inside = jnp.concatenate([inside] * comps, axis=1)
        field = jnp.concatenate([loads[c, :, nodes] for c in range(comps)], axis=1)
        own = jnp.concatenate([stiff[c : c + 1, nodes] for c in range(comps)], axis=1)
        r0[b] = field
        y0[b] = field * inside
        wide[b, :, : y0.shape[2]] = field * inside
        wide[b, :, y0.shape[2] :] = jnp.zeros((wide.shape[1], wide.shape[2] - y0.shape[2]), f32)
        mk[b] = inside
        dg[b] = own - shift


def split(matrix):
    high = matrix.astype(bf16)
    return high, (matrix - high.astype(f32)).astype(bf16)


def reverse_products(coupling, cols, y, acc, th=None):
    blocks, slots = coupling.shape[0], coupling.shape[1]
    acc[...] = jnp.zeros_like(acc)
    for r in range(blocks):
        ycat = parts_of(y[r])
        for k in range(slots):
            high, low = split(coupling[r, k])
            if th is not None:
                th[r, k] = high.T
            s = slot_of(cols, r, k, blocks)
            acc[s] += whole_of(plain_dot(ycat, high) + plain_dot(ycat, low))


def reverse_first(coupling, cols, y0, th, out_e, out_m, out_o, acc):
    blocks = y0.shape[0]
    reverse_products(coupling, cols, y0, acc, th)
    for b in range(blocks):
        out_e[b] = acc[b]
        out_m[b] = acc[blocks + b]
        out_o[b] = acc[2 * blocks + b]


def forward(th, source, cols, y, y_o, y_e, x, dg, mk, *rest, reverses):
    reverse, (result, *kept, xcat) = rest[:reverses], rest[reverses:]
    blocks, slots = th.shape[0], th.shape[1]
    for b in range(blocks):
        xcat[b] = parts_of(y_e[b])
        xcat[blocks + b] = parts_of(y[b])
        xcat[2 * blocks + b] = parts_of(y_o[b, :, : y.shape[2]])
    for r in range(blocks):
        total = jnp.zeros(xcat.shape[1:], f32)
        for k in range(slots):
            field = xcat[slot_of(cols, r, k, blocks)]
            low = source[r, k]
            if kept:
                low = split(low)[1].T
                kept[0][r, k] = low
            total += plain_dot(field, th[r, k]) + plain_dot(field, low)
        summed = whole_of(total)
        for part in reverse:
            summed += part[r, :, : y.shape[2]]
        result[r] = dg[r] * x[r] + mk[r] * summed


def reverse_second(coupling, cols, y1, r0, w, dg, out_e, out_m, out_o, grams, acc):
    blocks, n = y1.shape[0], y1.shape[1]
    total = jnp.zeros((2 * n, 3 * n), f32)
    for b in range(blocks):
        total += gram(
            jnp.concatenate([r0[b], w[b]], axis=0),
            jnp.concatenate([r0[b], w[b], dg[b] * w[b]], axis=0),
        )
    rest = jnp.zeros((n, grams.shape[1] - 4 * n), f32)
    grams[...] = jnp.concatenate([total[:n, : 2 * n], total[n:, n:], rest], axis=1)
    reverse_products(coupling, cols, y1, acc)
    for b in range(blocks):
        out_e[b] = acc[b]
        out_m[b] = acc[blocks + b]
        out_o[b] = jnp.zeros(out_o.shape[1:], f32)
        out_o[b, :, : y1.shape[2]] = acc[2 * blocks + b]


def cross_grams(out_e, out_m, out_o, y_e, y, y_o, grams, result):
    n, width = y.shape[1], y.shape[2]
    one = other = jnp.zeros((2 * n, 2 * n), f32)
    for b in range(y.shape[0]):
        for out, field in ((out_m, y), (out_e, y_e), (out_o, y_o)):
            sent, seen = parts_of(out[b, :, :width]), parts_of(field[b, :, :width])
            one += turned_dot(sent, seen)
            other += turned_dot(seen, sent)
    both = whole_of(one + other)
    cross = both[:, :n] + both[:, n:]
    before = jnp.zeros((n, 3 * n), f32)
    after = jnp.zeros((n, result.shape[1] - 4 * n), f32)
    result[...] = grams[...] + jnp.concatenate([before, cross, after], axis=1)


def eliminate(systems):
    count = systems[0][0].shape[0]
    rows = lax.broadcasted_iota(jnp.int32, (count, 128), 0)
    spread = [
        [jnp.broadcast_to(matrix[:, k : k + 1], (count, 128)) for k in range(count)]
        for matrix, _ in systems
    ]
    sides = [side for _, side in systems]
    for k in range(count):
        for i, columns in enumerate(spread):
            column = columns[k]
            scale = 1.0 / column[k : k + 1]

            def step(x):
                width = x.shape[1]
                pivot = x[k : k + 1] * scale[:, :width]
                return jnp.where(rows[:, :width] == k, pivot, x - column[:, :width] * pivot)

            spread[i] = [step(c) if j > k else c for j, c in enumerate(columns)]
            sides[i] = step(sides[i])
    return sides


def columns_of(matrix):
    return [matrix[:, k : k + 1] for k in range(matrix.shape[1])]


def small_dot(columns, right):
    terms = [column * right[k : k + 1, :] for k, column in enumerate(columns)]
    while len(terms) > 1:
        terms = [a + b for a, b in zip(terms[::2], terms[1::2])]
    return terms[0]


def finish(*refs, rounds, shift):
    gram_refs = refs[:rounds]
    r0, w, u, disp, resid = refs[rounds:]
    blocks, n = r0.shape[0], r0.shape[1]
    comps = disp.shape[0]
    bn = disp.shape[2] // blocks
    sums = gram_refs[0][...]
    for ref in gram_refs[1:]:
        sums += ref[:, : sums.shape[1]]
    h00, h01, h11, h12 = (sums[:, i * n : (i + 1) * n] for i in range(4))
    eye = (
        lax.broadcasted_iota(jnp.int32, (n, n), 0) == lax.broadcasted_iota(jnp.int32, (n, n), 1)
    ).astype(f32)
    first, inverse0 = eliminate(
        [(shift * h00 + h01, jnp.concatenate([h00, h01, eye], axis=1)), (h00, eye)]
    )
    step, keep, inverse = (first[:, i * n : (i + 1) * n] for i in range(3))
    c00, c01, c11, c12 = (columns_of(h) for h in (h00, h01, h11, h12))
    step_t, keep_t = small_dot(c00, inverse), small_dot(c01, inverse)
    h11s = small_dot(c11, step)
    past = h11s - small_dot(c01, keep)
    image = small_dot(c12, step) + shift * past - small_dot(c11, keep)
    onward = small_dot(columns_of(h11 + shift * h01), inverse0)
    both = small_dot(columns_of(step_t), jnp.concatenate([past, image, onward], axis=1))
    rho = both[:, :n]
    curvature = both[:, n : 2 * n] - small_dot(columns_of(both[:, 2 * n :]), rho)
    rho_columns = columns_of(rho)
    lead_t = keep_t + small_dot(rho_columns, inverse0)
    solved = eliminate([(curvature, jnp.concatenate([lead_t, step_t], axis=1))])[0]
    moved = small_dot(rho_columns, solved)
    lead_after, step_after = moved[:, :n], moved[:, n:]
    for_disp = (step_t + lead_after, -step_after)
    for_resid = (
        keep_t - shift * lead_after, shift * step_after - step_t - lead_after, step_after
    )
    for mix, out in ((for_disp, disp), (for_resid, resid)):
        mix_columns = [columns_of(m) for m in mix]
        for b in range(blocks):
            total = None
            for columns, x in zip(mix_columns, (r0, w, u)):
                for g in range(n):
                    term = columns[g] * x[b, g : g + 1, :]
                    total = term if total is None else total + term
            for c in range(comps):
                out[c, :, b * bn : (b + 1) * bn] = total[:, c * bn : (c + 1) * bn]


def widened(x):
    return jnp.pad(x, ((0, 0), (0, 0), (0, 64)))


def even_swap(x):
    count = lax.axis_size("row")
    return lax.ppermute(x, "row", [(i, i ^ 1) for i in range(count)])


def odd_swap(x):
    groups, count = lax.axis_size("groups"), lax.axis_size("row")
    route = []
    for g in range(groups):
        for i in range(count):
            if i == 0 or i == count - 1:
                other = g ^ 1 if (g ^ 1) < groups else g
                route.append((g * count + i, other * count + i))
            else:
                route.append((g * count + i, g * count + ((i + 1) ^ 1) - 1))
    return lax.ppermute(x, ("groups", "row"), route)


def swapped_sums(x):
    count = lax.axis_size("row")
    width = x.shape[1]
    base = 1
    while True:
        cross = 1 if base > 1 else 0
        masks = [base, 2 * base + cross, 3 * base + cross] if 2 * base < count else [base]
        got = []
        for i, mask in enumerate(masks):
            extra = (len(masks) - 1 - i) * width if base > 1 else 0
            sent = jnp.pad(x, ((0, 0), (0, extra))) if extra else x
            route = [(j, j ^ mask) for j in range(count)]
            got.append(lax.ppermute(sent, "row", route))
        base *= len(masks) + 1
        if base >= count:
            return [x, *got]
        x = x + sum(g[:, :width] for g in got)


def shards(coupling, columns, stiff_diag, interior, loads):
    blocks, slots, width = coupling.shape[0], coupling.shape[1], coupling.shape[2]
    fields, comps, nodes = loads.shape
    shift = slot_shift * slots + diag_middle
    flops = 8 * 2 * fields * blocks * slots * width * width
    field = jax.ShapeDtypeStruct((blocks, fields, width), f32)
    wide = jax.ShapeDtypeStruct((blocks, fields, width + 64), f32)
    row = jax.ShapeDtypeStruct((blocks, 1, width), f32)
    half = jax.ShapeDtypeStruct(coupling.shape, bf16)
    gram_shape = jax.ShapeDtypeStruct((fields, 128), f32)
    acc = pltpu.VMEM((3 * blocks, fields, width), f32)
    cat = pltpu.VMEM((3 * blocks, 2 * fields, width), bf16)

    r0, y0, wide0, dg, mk = call(
        lambda *refs: prepare(*refs, blocks=blocks, shift=diag_middle),
        (field, field, wide, row, row), [pl.BlockSpec(memory_space=pl.ANY)] * 3,
        [
            pltpu.VMEM((comps, fields, nodes), f32),
            pltpu.VMEM((nodes,), jnp.int32),
            pltpu.VMEM((comps, nodes), f32),
            pltpu.SemaphoreType.DMA((3,)),
        ],
        flops=10**10,
        name="prepare",
    )(*(in_hbm(x) for x in (loads.transpose(1, 0, 2), interior, stiff_diag)))
    y0_e, y0_o = even_swap(y0), odd_swap(wide0)
    th, a_e, a_m, a_o = call(
        reverse_first, (half, field, field, field), [vmem, smem, vmem],
        [acc], flops, name="reverse_first",
    )(coupling, columns, y0)
    b_e, b_o = even_swap(a_e), odd_swap(a_o)
    wp, tl = call(
        functools.partial(forward, reverses=1), (field, half), [vmem, vmem, smem] + [vmem] * 7,
        [cat], flops, name="forward_first",
    )(th, coupling, columns, y0, y0_o, y0_e, r0, dg, mk, a_m)
    w = wp + mk * (b_o + b_e)
    y1 = w * mk
    y1_e, y1_o = even_swap(y1), odd_swap(widened(y1))
    c_e, c_m, c_o, grams = call(
        reverse_second, (field, field, wide, gram_shape), [vmem, smem] + [vmem] * 4,
        [acc], flops, name="reverse_second",
    )(coupling, columns, y1, r0, w, dg)
    grams = call(cross_grams, gram_shape, [vmem] * 7, name="cross_grams")(
        c_e, c_m, c_o, y1_e, y1, y1_o, grams
    )
    sums = swapped_sums(grams)
    d_e, d_o = even_swap(c_e), odd_swap(c_o)
    u = call(
        functools.partial(forward, reverses=3), field, [vmem, vmem, smem] + [vmem] * 9,
        [cat], flops, name="forward_second",
    )(th, tl, columns, y1, y1_o, y1_e, w, dg, mk, c_m, d_o, d_e)
    out = jax.ShapeDtypeStruct((comps, fields, nodes), f32)
    disp, resid = call(
        lambda *refs: finish(*refs, rounds=len(sums), shift=shift),
        (out, out), [vmem] * (len(sums) + 3), name="finish",
    )(*sums, r0, w, u)
    return disp.transpose(1, 0, 2), resid.transpose(1, 0, 2)


def solution(mesh):
    placed = (
        P(("groups", "row"), None, None, None),
        P(("groups", "row"), None),
        P(None, ("groups", "row")),
        P(("groups", "row")),
        P(None, None, ("groups", "row")),
    )
    return jax.shard_map(
        shards,
        mesh=mesh,
        in_specs=placed,
        out_specs=(P(None, None, ("groups", "row")), P(None, None, ("groups", "row"))),
        check_vma=False,
    )
```

```python
import functools

import jax
import jax.numpy as jnp
from jax import lax
from jax.experimental import pallas as pl
from jax.experimental.pallas import tpu as pltpu
from jax.sharding import PartitionSpec as P

f32 = jnp.float32
bf16 = jnp.bfloat16
slot_shift = 1.2
diag_middle = 1.25


def call(body, out_shape, in_specs, scratch=(), flops=0, name=None, limit=24):
    return pl.pallas_call(
        body,
        out_shape=out_shape,
        in_specs=in_specs,
        out_specs=jax.tree.map(lambda _: pl.BlockSpec(memory_space=pltpu.VMEM), out_shape),
        scratch_shapes=list(scratch),
        compiler_params=pltpu.CompilerParams(vmem_limit_bytes=limit * 2**20),
        cost_estimate=pl.CostEstimate(flops=flops, bytes_accessed=2**20, transcendentals=0),
        name=name,
    )


vmem = pl.BlockSpec(memory_space=pltpu.VMEM)
smem = pl.BlockSpec(memory_space=pltpu.SMEM)


def in_hbm(x):
    return pltpu.with_memory_space_constraint(x, pltpu.HBM)


def thirds_of(x):
    high = x.astype(bf16).astype(f32)
    rest = x - high
    middle = rest.astype(bf16).astype(f32)
    return jnp.concatenate([high, middle, rest - middle], axis=0).astype(bf16)


def gram(left, right):
    a, b = left.shape[0], right.shape[0]
    parts = turned_dot(thirds_of(left), thirds_of(right))
    rows = parts[:a] + (parts[a : 2 * a] + parts[2 * a :])
    return rows[:, :b] + (rows[:, b : 2 * b] + rows[:, 2 * b :])


def parts_of(x):
    high = x.astype(bf16).astype(f32)
    return jnp.concatenate([high, x - high], axis=0).astype(bf16)


def whole_of(x16):
    half = x16.shape[0] // 2
    return x16[:half] + x16[half:]


def plain_dot(x, matrix):
    return lax.dot_general(x, matrix, (((1,), (0,)), ((), ())), preferred_element_type=f32)


def turned_dot(x, matrix):
    return lax.dot_general(x, matrix, (((1,), (1,)), ((), ())), preferred_element_type=f32)


def slot_of(cols, r, k, blocks):
    me = lax.axis_index("row")
    place = cols[r, k] - (me - 1) * blocks
    low = place < blocks
    high = place >= 2 * blocks
    swapped = jnp.where(low, place + 2 * blocks, jnp.where(high, place - 2 * blocks, place))
    return jnp.where(me % 2 == 0, swapped, place)


def prepare(
    loads_in, interior_in, stiff_in, r0, y0, wide, dg, mk, loads, interior, stiff, sems, *, blocks, shift
):
    comps = loads.shape[0]
    bn = loads.shape[2] // blocks
    fetches = [
        pltpu.make_async_copy(source, target, sems.at[i])
        for i, (source, target) in enumerate(
            ((loads_in, loads), (interior_in, interior), (stiff_in, stiff))
        )
    ]
    for fetch in fetches:
        fetch.start()
    for fetch in fetches:
        fetch.wait()
    inside_all = interior[...].astype(f32).reshape(1, -1)
    for b in range(blocks):
        nodes = pl.ds(b * bn, bn)
        inside = inside_all[:, b * bn : (b + 1) * bn]
        inside = jnp.concatenate([inside] * comps, axis=1)
        field = jnp.concatenate([loads[c, :, nodes] for c in range(comps)], axis=1)
        own = jnp.concatenate([stiff[c : c + 1, nodes] for c in range(comps)], axis=1)
        r0[b] = field
        y0[b] = field * inside
        wide[b, :, : y0.shape[2]] = field * inside
        wide[b, :, y0.shape[2] :] = jnp.zeros((wide.shape[1], wide.shape[2] - y0.shape[2]), f32)
        mk[b] = inside
        dg[b] = own - shift


def split(matrix):
    high = matrix.astype(bf16)
    return high, (matrix - high.astype(f32)).astype(bf16)


def reverse_products(coupling, cols, y, acc, th=None):
    blocks, slots = coupling.shape[0], coupling.shape[1]
    acc[...] = jnp.zeros_like(acc)
    for r in range(blocks):
        ycat = parts_of(y[r])
        for k in range(slots):
            high, low = split(coupling[r, k])
            if th is not None:
                th[r, k] = high.T
            s = slot_of(cols, r, k, blocks)
            acc[s] += whole_of(plain_dot(ycat, high) + plain_dot(ycat, low))


def reverse_first(coupling, cols, y0, th, out_e, out_m, out_o, acc):
    blocks = y0.shape[0]
    reverse_products(coupling, cols, y0, acc, th)
    for b in range(blocks):
        out_e[b] = acc[b]
        out_m[b] = acc[blocks + b]
        out_o[b] = acc[2 * blocks + b]


def forward(th, source, cols, y, y_o, y_e, x, dg, mk, *rest, reverses):
    reverse, (result, *kept, xcat) = rest[:reverses], rest[reverses:]
    blocks, slots = th.shape[0], th.shape[1]
    for b in range(blocks):
        xcat[b] = parts_of(y_e[b])
        xcat[blocks + b] = parts_of(y[b])
        xcat[2 * blocks + b] = parts_of(y_o[b, :, : y.shape[2]])
    for r in range(blocks):
        total = jnp.zeros(xcat.shape[1:], f32)
        for k in range(slots):
            field = xcat[slot_of(cols, r, k, blocks)]
            low = source[r, k]
            if kept:
                low = split(low)[1].T
                kept[0][r, k] = low
            total += plain_dot(field, th[r, k]) + plain_dot(field, low)
        summed = whole_of(total)
        for part in reverse:
            summed += part[r, :, : y.shape[2]]
        result[r] = dg[r] * x[r] + mk[r] * summed


def reverse_second(coupling, cols, y1, r0, w, dg, out_e, out_m, out_o, grams, acc):
    blocks, n = y1.shape[0], y1.shape[1]
    total = jnp.zeros((2 * n, 3 * n), f32)
    for b in range(blocks):
        total += gram(
            jnp.concatenate([r0[b], w[b]], axis=0),
            jnp.concatenate([r0[b], w[b], dg[b] * w[b]], axis=0),
        )
    rest = jnp.zeros((n, grams.shape[1] - 4 * n), f32)
    grams[...] = jnp.concatenate([total[:n, : 2 * n], total[n:, n:], rest], axis=1)
    reverse_products(coupling, cols, y1, acc)
    for b in range(blocks):
        out_e[b] = acc[b]
        out_m[b] = acc[blocks + b]
        out_o[b] = jnp.zeros(out_o.shape[1:], f32)
        out_o[b, :, : y1.shape[2]] = acc[2 * blocks + b]


def cross_grams(out_e, out_m, out_o, y_e, y, y_o, grams, result):
    n, width = y.shape[1], y.shape[2]
    one = other = jnp.zeros((2 * n, 2 * n), f32)
    for b in range(y.shape[0]):
        for out, field in ((out_m, y), (out_e, y_e), (out_o, y_o)):
            sent, seen = parts_of(out[b, :, :width]), parts_of(field[b, :, :width])
            one += turned_dot(sent, seen)
            other += turned_dot(seen, sent)
    both = whole_of(one + other)
    cross = both[:, :n] + both[:, n:]
    before = jnp.zeros((n, 3 * n), f32)
    after = jnp.zeros((n, result.shape[1] - 4 * n), f32)
    result[...] = grams[...] + jnp.concatenate([before, cross, after], axis=1)


def eliminate(systems):
    count = systems[0][0].shape[0]
    rows = lax.broadcasted_iota(jnp.int32, (count, 128), 0)
    spread = [
        [jnp.broadcast_to(matrix[:, k : k + 1], (count, 128)) for k in range(count)]
        for matrix, _ in systems
    ]
    sides = [side for _, side in systems]
    for k in range(count):
        for i, columns in enumerate(spread):
            column = columns[k]
            scale = 1.0 / column[k : k + 1]

            def step(x):
                width = x.shape[1]
                pivot = x[k : k + 1] * scale[:, :width]
                return jnp.where(rows[:, :width] == k, pivot, x - column[:, :width] * pivot)

            spread[i] = [step(c) if j > k else c for j, c in enumerate(columns)]
            sides[i] = step(sides[i])
    return sides


def columns_of(matrix):
    return [matrix[:, k : k + 1] for k in range(matrix.shape[1])]


def small_dot(columns, right):
    terms = [column * right[k : k + 1, :] for k, column in enumerate(columns)]
    while len(terms) > 1:
        terms = [a + b for a, b in zip(terms[::2], terms[1::2])]
    return terms[0]


def finish(*refs, rounds, shift):
    gram_refs = refs[:rounds]
    r0, w, u, disp, resid = refs[rounds:]
    blocks, n = r0.shape[0], r0.shape[1]
    comps = disp.shape[0]
    bn = disp.shape[2] // blocks
    sums = gram_refs[0][...]
    for ref in gram_refs[1:]:
        sums += ref[:, : sums.shape[1]]
    h00, h01, h11, h12 = (sums[:, i * n : (i + 1) * n] for i in range(4))
    eye = (
        lax.broadcasted_iota(jnp.int32, (n, n), 0) == lax.broadcasted_iota(jnp.int32, (n, n), 1)
    ).astype(f32)
    first, inverse0 = eliminate(
        [(shift * h00 + h01, jnp.concatenate([h00, h01, eye], axis=1)), (h00, eye)]
    )
    step, keep, inverse = (first[:, i * n : (i + 1) * n] for i in range(3))
    c00, c01, c11, c12 = (columns_of(h) for h in (h00, h01, h11, h12))
    step_t, keep_t = small_dot(c00, inverse), small_dot(c01, inverse)
    h11s = small_dot(c11, step)
    past = h11s - small_dot(c01, keep)
    image = small_dot(c12, step) + shift * past - small_dot(c11, keep)
    onward = small_dot(columns_of(h11 + shift * h01), inverse0)
    both = small_dot(columns_of(step_t), jnp.concatenate([past, image, onward], axis=1))
    rho = both[:, :n]
    curvature = both[:, n : 2 * n] - small_dot(columns_of(both[:, 2 * n :]), rho)
    rho_columns = columns_of(rho)
    lead_t = keep_t + small_dot(rho_columns, inverse0)
    solved = eliminate([(curvature, jnp.concatenate([lead_t, step_t], axis=1))])[0]
    moved = small_dot(rho_columns, solved)
    lead_after, step_after = moved[:, :n], moved[:, n:]
    for_disp = (step_t + lead_after, -step_after)
    for_resid = (
        keep_t - shift * lead_after, shift * step_after - step_t - lead_after, step_after
    )
    for mix, out in ((for_disp, disp), (for_resid, resid)):
        mix_columns = [columns_of(m) for m in mix]
        for b in range(blocks):
            total = None
            for columns, x in zip(mix_columns, (r0, w, u)):
                for g in range(n):
                    term = columns[g] * x[b, g : g + 1, :]
                    total = term if total is None else total + term
            for c in range(comps):
                out[c, :, b * bn : (b + 1) * bn] = total[:, c * bn : (c + 1) * bn]


def widened(x):
    return jnp.pad(x, ((0, 0), (0, 0), (0, 64)))


def even_swap(x):
    count = lax.axis_size("row")
    return lax.ppermute(x, "row", [(i, i ^ 1) for i in range(count)])


def odd_swap(x):
    groups, count = lax.axis_size("groups"), lax.axis_size("row")
    route = []
    for g in range(groups):
        for i in range(count):
            if i == 0 or i == count - 1:
                other = g ^ 1 if (g ^ 1) < groups else g
                route.append((g * count + i, other * count + i))
            else:
                route.append((g * count + i, g * count + ((i + 1) ^ 1) - 1))
    return lax.ppermute(x, ("groups", "row"), route)


def swapped_sums(x):
    count = lax.axis_size("row")
    width = x.shape[1]
    base = 1
    while True:
        cross = 1 if base > 1 else 0
        masks = [base + cross, 2 * base, 3 * base + cross] if 2 * base < count else [base]
        got = []
        for i, mask in enumerate(masks):
            extra = (len(masks) - 1 - i) * width if base > 1 else 0
            sent = jnp.pad(x, ((0, 0), (0, extra))) if extra else x
            route = [(j, j ^ mask) for j in range(count)]
            got.append(lax.ppermute(sent, "row", route))
        base *= len(masks) + 1
        if base >= count:
            return [x, *got]
        x = x + sum(g[:, :width] for g in got)


def shards(coupling, columns, stiff_diag, interior, loads):
    blocks, slots, width = coupling.shape[0], coupling.shape[1], coupling.shape[2]
    fields, comps, nodes = loads.shape
    shift = slot_shift * slots + diag_middle
    flops = 8 * 2 * fields * blocks * slots * width * width
    field = jax.ShapeDtypeStruct((blocks, fields, width), f32)
    wide = jax.ShapeDtypeStruct((blocks, fields, width + 64), f32)
    row = jax.ShapeDtypeStruct((blocks, 1, width), f32)
    half = jax.ShapeDtypeStruct(coupling.shape, bf16)
    gram_shape = jax.ShapeDtypeStruct((fields, 128), f32)
    acc = pltpu.VMEM((3 * blocks, fields, width), f32)
    cat = pltpu.VMEM((3 * blocks, 2 * fields, width), bf16)

    r0, y0, wide0, dg, mk = call(
        lambda *refs: prepare(*refs, blocks=blocks, shift=diag_middle),
        (field, field, wide, row, row), [pl.BlockSpec(memory_space=pl.ANY)] * 3,
        [
            pltpu.VMEM((comps, fields, nodes), f32),
            pltpu.VMEM((nodes,), jnp.int32),
            pltpu.VMEM((comps, nodes), f32),
            pltpu.SemaphoreType.DMA((3,)),
        ],
        flops=10**10,
        name="prepare",
    )(*(in_hbm(x) for x in (loads.transpose(1, 0, 2), interior, stiff_diag)))
    y0_e, y0_o = even_swap(y0), odd_swap(wide0)
    th, a_e, a_m, a_o = call(
        reverse_first, (half, field, field, field), [vmem, smem, vmem],
        [acc], flops, name="reverse_first",
    )(coupling, columns, y0)
    b_e, b_o = even_swap(a_e), odd_swap(a_o)
    wp, tl = call(
        functools.partial(forward, reverses=1), (field, half), [vmem, vmem, smem] + [vmem] * 7,
        [cat], flops, name="forward_first",
    )(th, coupling, columns, y0, y0_o, y0_e, r0, dg, mk, a_m)
    w = wp + mk * (b_o + b_e)
    y1 = w * mk
    y1_e, y1_o = even_swap(y1), odd_swap(widened(y1))
    c_e, c_m, c_o, grams = call(
        reverse_second, (field, field, wide, gram_shape), [vmem, smem] + [vmem] * 4,
        [acc], flops, name="reverse_second",
    )(coupling, columns, y1, r0, w, dg)
    grams = call(cross_grams, gram_shape, [vmem] * 7, name="cross_grams")(
        c_e, c_m, c_o, y1_e, y1, y1_o, grams
    )
    sums = swapped_sums(grams)
    d_e, d_o = even_swap(c_e), odd_swap(c_o)
    u = call(
        functools.partial(forward, reverses=3), field, [vmem, vmem, smem] + [vmem] * 9,
        [cat], flops, name="forward_second",
    )(th, tl, columns, y1, y1_o, y1_e, w, dg, mk, c_m, d_o, d_e)
    out = jax.ShapeDtypeStruct((comps, fields, nodes), f32)
    disp, resid = call(
        lambda *refs: finish(*refs, rounds=len(sums), shift=shift),
        (out, out), [vmem] * (len(sums) + 3), name="finish",
    )(*sums, r0, w, u)
    return disp.transpose(1, 0, 2), resid.transpose(1, 0, 2)


def solution(mesh):
    placed = (
        P(("groups", "row"), None, None, None),
        P(("groups", "row"), None),
        P(None, ("groups", "row")),
        P(("groups", "row")),
        P(None, None, ("groups", "row")),
    )
    return jax.shard_map(
        shards,
        mesh=mesh,
        in_specs=placed,
        out_specs=(P(None, None, ("groups", "row")), P(None, None, ("groups", "row"))),
        check_vma=False,
    )
```
